32 devices in a mesh: flow: 8 (over z, y), group: 4 (over x, core).
Axes of the slice: x: 2, y: 2, z: 4, core: 2. Of those that a mesh axis runs over, the one named last changes fastest.
Arguments:
- cell_state: float32 [12, 262144], P(None, 'flow'), may hold values from 0.1 to 10
- inflow: float32 [12, 2048], P(None, ('flow', 'group')), may hold values from 0.1 to 10
- courant: float32 [256, 2048], P(None, ('flow', 'group')), may hold values from 1 to 15360
- pick: int32 [4, 8, 8, 2048], P('group', 'flow'), may hold values from 0 to 32767, as said below
- node_slot: int32 [256, 2048], P(None, ('flow', 'group')), may hold values from 0 to 16383, as said below
- stoich: float32 [6, 12], replicated, may hold values from 0 to 0.25
- logk: float32 [6], replicated, may hold values from -3 to 0
Outputs:
- cell_species: float32 [18, 262144], P(None, ('flow', 'group'))
The draws below stay inside these ranges and needn't reach their ends.
Inputs may be any that keep to these rules, and one draw needn't show every extreme that they name: pick[g, a, b, k] lies in the block of 128 local cells numbered ((b * 2048 + k) // 128 + g * 128) modulo (256). With j = s % 64, node_slot[n, s] lies in the tile of 128 records numbered (n * 64 + j) // 128.
All inputs are finite; a program needn't handle non-finite values.
Results may differ from the reference program's by a relative error of at most 0.00011.
Values sent between devices are 32-bit elements; how exact they have to be, the bound alone decides.
A program may use at most 128 MiB of HBM per device.

```python
import math
import jax
import jax.numpy as jnp
from jax import lax

NC = 12
NX = 6
NODES = 256
ITERS = 4
WIN = 128
SL_DEV = 64
CELL_DEV = 32768
SLOTS = 16384
CAP = 2048
SL = 2048
CELLS = 262144
N_FLOW = 8
N_GROUP = 4


def draw_courant(key, part):
    key = jax.random.fold_in(key, 7)
    first, second = jax.random.split(key)
    lowest = math.log(2.0)
    speed = jnp.exp(jax.random.uniform(first, (1, SL), jnp.float32, lowest, math.log(30.0 * NODES)))
    rough = jax.random.uniform(second, (NODES, SL), jnp.float32, 0.5, 2.0)
    return (speed * rough).astype(jnp.float32)


def draw_pick(key, part):
    key = jax.random.fold_in(key, 11)
    shape = (N_GROUP, N_FLOW, N_FLOW, CAP)
    group_ids = jax.lax.broadcasted_iota(jnp.int32, shape, 0)
    target = jax.lax.broadcasted_iota(jnp.int32, shape, 2)
    record = jax.lax.broadcasted_iota(jnp.int32, shape, 3)
    tiles = (target * CAP + record) // WIN
    blocks = (tiles + group_ids * (SLOTS // WIN)) % (CELL_DEV // WIN)
    inside = jax.random.randint(key, shape, 0, WIN, dtype=jnp.int32)
    return (blocks * WIN + inside).astype(jnp.int32)


def draw_node_slot(key, part):
    key = jax.random.fold_in(key, 13)
    shape = (NODES, SL)
    node_ids = jax.lax.broadcasted_iota(jnp.int32, shape, 0)
    line_ids = jax.lax.broadcasted_iota(jnp.int32, shape, 1)
    tiles = (node_ids * SL_DEV + line_ids % SL_DEV) // WIN
    inside = jax.random.randint(key, shape, 0, WIN, dtype=jnp.int32)
    return (tiles * WIN + inside).astype(jnp.int32)


def shard_levels(stream_key, extent, cuts, least, high):
    def one(axis_at, shards_of):
        draws = jax.random.uniform(jax.random.fold_in(jax.random.fold_in(stream_key, 6), axis_at), (shards_of,), jnp.float32, least / len(cuts), high / len(cuts))
        return jnp.repeat(jnp.exp(draws), extent[axis_at] // shards_of).reshape((-1,) + (1,) * (len(extent) - axis_at - 1))

    loudness = one(*cuts[0])
    for cut in cuts[1:]:
        loudness = loudness * one(*cut)
    return loudness


def setup_inputs(seed: int = 0) -> dict:
    key_of = jax.random.split(jax.random.key(seed), 8)
    cell_state = jnp.clip(jnp.exp(math.log(10.0) - 4.6051702 * jax.random.uniform(key_of[0], (NC, CELLS), jnp.float32) ** shard_levels(key_of[0], (NC, CELLS), ((1, 8),), -0.2, 0.2)), 0.1, 10.0)
    inflow = jnp.clip(jnp.exp(math.log(10.0) - 4.6051702 * jax.random.uniform(key_of[1], (NC, SL), jnp.float32) ** shard_levels(key_of[1], (NC, SL), ((1, 32),), -0.2, 0.2)), 0.1, 10.0)
    courant = draw_courant(jax.random.fold_in(key_of[7], 71), 0)
    pick = draw_pick(jax.random.fold_in(key_of[7], 71), 0)
    node_slot = draw_node_slot(jax.random.fold_in(key_of[7], 71), 0)
    stoich = jnp.clip(jax.random.uniform(key_of[5], (NX, NC), jnp.float32, 0.0, 0.25), 0.0, 0.25)
    logk = jnp.clip(jax.random.uniform(key_of[6], (NX,), jnp.float32, -3.0, 0.0), -3.0, 0.0)
    return dict(cell_state=cell_state, inflow=inflow, courant=courant, pick=pick, node_slot=node_slot, stoich=stoich, logk=logk)


def solve_spd(matrix, rhs):
    order = len(rhs)
    lower = {}
    inverse = []
    for outer in range(order):
        for inner in range(outer + 1):
            total = matrix[outer, inner]
            for other in range(inner):
                total = total - lower[outer, other] * lower[inner, other]
            if outer == inner:
                inverse.append(lax.rsqrt(total))
            else:
                lower[outer, inner] = total * inverse[inner]
    middle = []
    for outer in range(order):
        total = rhs[outer]
        for other in range(outer):
            total = total - lower[outer, other] * middle[other]
        middle.append(total * inverse[outer])
    result = [None] * order
    for outer in reversed(range(order)):
        total = middle[outer]
        for other in range(outer + 1, order):
            total = total - lower[other, outer] * result[other]
        result[outer] = total * inverse[outer]
    return result

def speciate(totals, stoich, logk):
    count_comp = totals.shape[0]
    identity = jnp.eye(count_comp, dtype=jnp.float32)
    logfree = jnp.log(totals)
    for sweep in range(ITERS):
        free = jnp.exp(logfree)
        complexes = jnp.exp(logk[:, None] + jnp.dot(stoich, logfree, precision=lax.Precision.HIGHEST, preferred_element_type=jnp.float32))
        mismatch = free + jnp.dot(stoich.T, complexes, precision=lax.Precision.HIGHEST, preferred_element_type=jnp.float32) - totals
        jacobian = jnp.einsum('pi,pj,pn->ijn', stoich, stoich, complexes, precision=lax.Precision.HIGHEST)
        jacobian = jacobian + identity[:, :, None] * free[:, None, :]
        update = solve_spd(jacobian, [-mismatch[comp] for comp in range(count_comp)])
        logfree = logfree + jnp.stack(update)
    complexes = jnp.exp(logk[:, None] + jnp.dot(stoich, logfree, precision=lax.Precision.HIGHEST, preferred_element_type=jnp.float32))
    return jnp.concatenate([jnp.exp(logfree), complexes], axis=0)

def reference(cell_state, inflow, courant, pick, node_slot, stoich, logk):
    count_comp = cell_state.shape[0]
    line_ids = lax.broadcasted_iota(jnp.int32, (NODES, SL), 1)
    device_id = (line_ids // SL_DEV).astype(jnp.int32)
    flow_id = (device_id // N_GROUP).astype(jnp.int32)
    group_id = (device_id % N_GROUP).astype(jnp.int32)
    anchor = (node_slot // CAP).astype(jnp.int32)
    record = (node_slot % CAP).astype(jnp.int32)
    cell = (anchor * CELL_DEV + pick[group_id, anchor, flow_id, record]).astype(jnp.int32)
    old = cell_state[:, cell]
    weight = courant / (1.0 + courant)
    source = old / (1.0 + courant)[None]

    def advance(carry, inputs):
        node_weight, node_source = inputs
        moved = node_weight[None] * carry + node_source
        return (moved, moved)
    last, moved = lax.scan(advance, inflow, (weight, jnp.transpose(source, (1, 0, 2))))
    moved = jnp.transpose(moved, (1, 0, 2))
    devices = SL // SL_DEV
    blocks = moved.reshape(count_comp, NODES, devices, SL_DEV)
    blocks = jnp.transpose(blocks, (2, 0, 1, 3)).reshape(devices, count_comp, NODES * SL_DEV)
    species = lax.map(lambda block: speciate(block, stoich, logk), blocks)
    width = species.shape[1]
    species = species.reshape(devices, width, NODES, SL_DEV)
    species = jnp.transpose(species, (1, 2, 0, 3)).reshape(width, NODES * SL)
    flat_cell = cell.reshape(-1)
    totals = jnp.zeros((width, CELLS), jnp.float32).at[:, flat_cell].add(species)
    counts = jnp.zeros((CELLS,), jnp.float32).at[flat_cell].add(jnp.ones((NODES * SL,), jnp.float32))
    return totals / jnp.maximum(counts, 1.0)[None]
```

```python
import functools

import jax
import jax.numpy as jnp
from jax import lax
from jax.experimental import pallas as pl
from jax.experimental.pallas import tpu as pltpu
from jax.sharding import PartitionSpec as P

ITERS = 4
WIN = 128
LIMIT = 56 * 1024 * 1024
MESH = pl.DeviceIdType.MESH


def blend(factors, values):
    total = factors[0] * values[0]
    for factor, value in zip(factors[1:], values[1:]):
        total = total + factor * value
    return total


def factor_and_solve(matrix, rhs):
    order = len(rhs)
    lower, inverse, middle = {}, [], []
    for p in range(order):
        for r in range(p + 1):
            total = matrix(p, r)
            for o in range(r):
                total = total - lower[p, o] * lower[r, o]
            if p == r:
                inverse.append(lax.rsqrt(total))
            else:
                lower[p, r] = total * inverse[r]
        total = rhs[p]
        for o in range(p):
            total = total - lower[p, o] * middle[o]
        middle.append(total * inverse[p])
    value = [None] * order
    for p in reversed(range(order)):
        total = middle[p]
        for o in range(p + 1, order):
            total = total - lower[o, p] * value[o]
        value[p] = total * inverse[p]
    return value


def newton(totals, stoich, pairs, logk):
    comps, plexes = len(totals), len(logk)
    columns = [[stoich[p][c] for p in range(plexes)] for c in range(comps)]
    logfree = [jnp.log(t) for t in totals]
    over = [1.0 / t for t in totals]
    backs = [jnp.exp(-(logk[p] + blend(stoich[p], logfree))) for p in range(plexes)]

    def small(p, r):
        total = blend(pairs[p, r], over)
        return total + backs[p] if p == r else total

    value = factor_and_solve(small, [jnp.ones_like(totals[0])] * plexes)
    logfree = [x - o * blend(s, value) for x, o, s in zip(logfree, over, columns)]
    for sweep in range(1, ITERS):
        free = [jnp.exp(x) for x in logfree]
        roots = [jnp.exp(0.5 * (logk[p] + blend(stoich[p], logfree))) for p in range(plexes)]
        mixed = [[s[p] * roots[p] for p in range(plexes)] for s in columns]
        rhs = [f + blend(m, roots) - t for f, m, t in zip(free, mixed, totals)]

        def full(p, r):
            total = blend(mixed[p], mixed[r])
            return total + free[p] if p == r else total

        update = factor_and_solve(full, rhs)
        logfree = [x - u for x, u in zip(logfree, update)]
    plex = [jnp.exp(logk[p] + blend(stoich[p], logfree)) for p in range(plexes)]
    return [jnp.exp(x) for x in logfree] + plex


def forward_kernel(
    sizes,
    stoich_ref,
    state_ref,
    pick_ref,
    slot_ref,
    courant_ref,
    cells_ref,
    picks_ref,
    slots_ref,
    weight_ref,
    scale_ref,
    pairs_ref,
    table_ref,
    turned_ref,
    index_ref,
    own_sem,
    send_sem,
    recv_sem,
    pick_send,
    pick_recv,
):
    flow_count, group_count, parts, members, capacity = sizes
    flow, group = lax.axis_index("flow"), lax.axis_index("group")
    part, rank = lax.rem(group, parts), lax.div(group, parts)
    records = flow_count * capacity
    piece = capacity // members
    others = [
        (flow, lax.rem(rank + m, members) * parts + part) for m in range(1, members)
    ]
    peers = [(lax.rem(flow + d, flow_count), group) for d in range(1, flow_count)]
    barrier = pltpu.get_barrier_semaphore()
    for peer in others + peers:
        pl.semaphore_signal(barrier, inc=1, device_id=peer, device_id_type=MESH)
    per = capacity // WIN
    for k in range(per):
        table_ref[pl.ds(k, flow_count, stride=per), :] = pick_ref[:, k * WIN : (k + 1) * WIN]
    pl.semaphore_wait(barrier, len(others) + len(peers))

    def cut(start, size):
        return pl.ds(pl.multiple_of(start, WIN), size)

    def rows(index):
        return pl.ds(pl.multiple_of(index * per, per), per)

    first = part * records
    for d in range(1, flow_count):
        peer = peers[d - 1]
        pltpu.make_async_remote_copy(
            src_ref=state_ref.at[:, cut(first + peer[0] * capacity + rank * piece, piece)],
            dst_ref=cells_ref.at[:, cut(flow * capacity + rank * piece, piece)],
            send_sem=send_sem.at[0, d],
            recv_sem=recv_sem.at[0, d],
            device_id=peer,
            device_id_type=MESH,
        ).start()
    for d in range(1, flow_count):
        peer = peers[d - 1]
        pltpu.make_async_remote_copy(
            src_ref=table_ref.at[rows(peer[0])],
            dst_ref=picks_ref.at[rows(flow)],
            send_sem=pick_send.at[d],
            recv_sem=pick_recv.at[d],
            device_id=peer,
            device_id_type=MESH,
        ).start()
    mine = [
        pltpu.make_async_copy(
            state_ref.at[:, cut(first + flow * capacity, capacity)],
            cells_ref.at[:, cut(flow * capacity, capacity)],
            own_sem.at[0],
        ),
        pltpu.make_async_copy(table_ref.at[rows(flow)], picks_ref.at[rows(flow)], own_sem.at[1]),
    ]
    for copy in mine:
        copy.start()

    plexes, comps = stoich_ref.shape
    for p in range(plexes):
        for r in range(p + 1):
            for c in range(comps):
                pairs_ref[(p * plexes + r) * comps + c] = stoich_ref[p, c] * stoich_ref[r, c]
    tiles = records // WIN
    left = lax.broadcasted_iota(jnp.int32, (tiles, WIN), 1) < WIN // 2

    def by_tile(ref, view):
        value = ref[...]
        view[...] = jnp.transpose(jnp.concatenate([value, value], axis=0))
        even = view[pl.ds(0, tiles, stride=2), :]
        odd = view[pl.ds(1, tiles, stride=2), :]
        return jnp.where(left, even, odd)

    courant = by_tile(courant_ref, turned_ref)
    scale = 1.0 / (1.0 + courant)
    scale_ref[...] = scale
    weight_ref[...] = courant * scale
    slots_ref[...] = by_tile(slot_ref, index_ref) & (WIN - 1)

    def arrival(d, m):
        source = lax.rem(flow + flow_count - d, flow_count)
        owner = lax.rem(rank + members - m, members)
        span = cut(source * capacity + owner * piece, piece)
        return pltpu.make_async_remote_copy(
            src_ref=cells_ref.at[:, span],
            dst_ref=cells_ref.at[:, span],
            send_sem=send_sem.at[m, d],
            recv_sem=recv_sem.at[m, d],
            device_id=others[m - 1] if m else peers[d - 1],
            device_id_type=MESH,
        )

    for d in range(1, flow_count):
        arrival(d, 0).wait_recv()
        source = lax.rem(flow + flow_count - d, flow_count)
        span = cut(source * capacity + rank * piece, piece)
        for m in range(1, members):
            pltpu.make_async_remote_copy(
                src_ref=cells_ref.at[:, span],
                dst_ref=cells_ref.at[:, span],
                send_sem=send_sem.at[m, d],
                recv_sem=recv_sem.at[m, d],
                device_id=others[m - 1],
                device_id_type=MESH,
            ).start()
    for copy in mine:
        copy.wait()
    for d in range(1, flow_count):
        source = lax.rem(flow + flow_count - d, flow_count)
        pltpu.make_async_remote_copy(
            src_ref=table_ref.at[rows(peers[d - 1][0])],
            dst_ref=picks_ref.at[rows(source)],
            send_sem=pick_send.at[d],
            recv_sem=pick_recv.at[d],
            device_id=peers[d - 1],
            device_id_type=MESH,
        ).wait()
        arrival(d, 0).wait_send()
        for m in range(1, members):
            arrival(d, m).wait()


def forward(stoich, state, pick, slot, courant, sizes):
    flow_count, group_count, parts, members, capacity = sizes
    plexes, comps = stoich.shape
    records = flow_count * capacity
    tiles = records // WIN
    anywhere = pl.BlockSpec(memory_space=pl.ANY)
    vmem = pl.BlockSpec(memory_space=pltpu.VMEM)
    smem = pl.BlockSpec(memory_space=pltpu.SMEM)
    table = jax.ShapeDtypeStruct((tiles, WIN), jnp.float32)
    whole = jax.ShapeDtypeStruct((tiles, WIN), jnp.int32)
    return pl.pallas_call(
        functools.partial(forward_kernel, sizes),
        out_shape=(
            jax.ShapeDtypeStruct((comps, records), jnp.float32),
            whole,
            whole,
            table,
            table,
            jax.ShapeDtypeStruct((plexes * plexes * comps,), jnp.float32),
        ),
        in_specs=[smem, anywhere, vmem, vmem, vmem],
        out_specs=(vmem, vmem, vmem, vmem, vmem, smem),
        scratch_shapes=[
            pltpu.VMEM((tiles, WIN), jnp.int32),
            pltpu.VMEM((2 * tiles, WIN), jnp.float32),
            pltpu.VMEM((2 * tiles, WIN), jnp.int32),
            pltpu.SemaphoreType.DMA((2,)),
            pltpu.SemaphoreType.DMA((members, flow_count)),
            pltpu.SemaphoreType.DMA((members, flow_count)),
            pltpu.SemaphoreType.DMA((flow_count,)),
            pltpu.SemaphoreType.DMA((flow_count,)),
        ],
        compiler_params=pltpu.CompilerParams(
            collective_id=0, has_side_effects=True, vmem_limit_bytes=LIMIT
        ),
    )(stoich, state, pick, slot, courant)


def react_kernel(
    sizes,
    stoich_ref,
    pairs_ref,
    logk_ref,
    cells_ref,
    pick_ref,
    slot_ref,
    weight_ref,
    scale_ref,
    inflow_ref,
    out_ref,
    where_ref,
    moved_ref,
    species_ref,
    sums_ref,
    pair_ref,
    own_sem,
    pair_send,
    pair_recv,
    send_sem,
    recv_sem,
):
    flow_count, group_count, parts, members, capacity = sizes
    comps = cells_ref.shape[0]
    plexes = logk_ref.shape[0]
    width = comps + plexes
    tall = species_ref.shape[0] // (capacity // WIN)
    tiles = pick_ref.shape[0]
    per = capacity // WIN
    half = WIN // 2
    deep = moved_ref.shape[0] // tiles

    flow, group = lax.axis_index("flow"), lax.axis_index("group")
    part, rank = lax.rem(group, parts), lax.div(group, parts)
    share = flow_count * parts // group_count

    def chief_of(which):
        return which * members // parts

    chief = chief_of(part)
    spot = lax.rem(rank + members - chief, members)
    target = part * members + lax.div(flow, share)
    sender = lax.div(group, members)
    sender_group = chief_of(sender) * parts + sender
    sender_flow = lax.rem(group, members) * share
    place = lax.rem(flow, share)

    def column(s):
        return lax.rem(flow + 1 + s, flow_count)

    def to_chief(s, index):
        return pltpu.make_async_remote_copy(
            src_ref=sums_ref.at[column(s)],
            dst_ref=pair_ref.at[index, column(s)],
            send_sem=pair_send.at[s],
            recv_sem=pair_recv.at[index, s],
            device_id=(flow, chief * parts + part),
            device_id_type=MESH,
        )

    def to_owner(s, spot_there):
        return pltpu.make_async_remote_copy(
            src_ref=pair_ref.at[0, column(s)],
            dst_ref=out_ref.at[spot_there],
            send_sem=send_sem.at[s],
            recv_sem=recv_sem.at[spot_there],
            device_id=(column(s), target),
            device_id_type=MESH,
        )

    barrier = pltpu.get_barrier_semaphore()
    for k in range(share):
        source = sender_flow + k

        @pl.when(jnp.logical_or(source != flow, sender_group != group))
        def _():
            pl.semaphore_signal(
                barrier, inc=1, device_id=(source, sender_group), device_id_type=MESH
            )

    @pl.when(spot == 0)
    def _():
        for m in range(1, members):
            pl.semaphore_signal(
                barrier,
                inc=1,
                device_id=(flow, lax.rem(chief + m, members) * parts + part),
                device_id_type=MESH,
            )

    where_ref[...] = jnp.take_along_axis(pick_ref[...] & (WIN - 1), slot_ref[...], axis=1)
    left = lax.broadcasted_iota(jnp.int32, (deep, WIN), 1) < half
    zero = jnp.zeros((deep, WIN), jnp.float32)
    inflow = jnp.concatenate([inflow_ref[...], inflow_ref[...]], axis=1)
    inflow = jnp.concatenate([inflow, zero[comps:]], axis=0)

    def transport(t, carry):
        before_w, before_s, moved = carry
        span = pl.ds(pl.multiple_of(t * WIN, WIN), WIN)
        index = jnp.broadcast_to(where_ref[pl.ds(t, 1), :], (deep, WIN))
        block = jnp.concatenate([cells_ref[:, span], zero[comps:]], axis=0)
        old = jnp.take_along_axis(block, index, axis=1)
        weight = jnp.broadcast_to(weight_ref[pl.ds(t, 1), :], (deep, WIN))
        source = old * jnp.broadcast_to(scale_ref[pl.ds(t, 1), :], (deep, WIN))
        turned_w = pltpu.roll(weight, half, 1)
        turned_s = pltpu.roll(source, half, 1)
        both = weight * jnp.where(left, before_w, turned_w)
        added = weight * jnp.where(left, before_s, turned_s) + source
        moved = both * moved + added
        moved_ref[pl.ds(pl.multiple_of(t * deep, deep), deep), :] = moved
        return turned_w, turned_s, moved

    lax.fori_loop(0, tiles, transport, (zero + 1.0, zero, inflow), unroll=8)

    stoich = [[stoich_ref[p, c] for c in range(comps)] for p in range(plexes)]
    logk = [logk_ref[p] for p in range(plexes)]
    pairs = {}
    for p in range(plexes):
        for r in range(p + 1):
            base = (p * plexes + r) * comps
            pairs[p, r] = [pairs_ref[base + c] for c in range(comps)]
    species_ref[...] = jnp.ones_like(species_ref)
    lanes = lax.broadcasted_iota(jnp.int32, (WIN, WIN), 0)

    def deposit(s):
        for row in range(per):
            value = species_ref[row * tall : (row + 1) * tall, :]
            high = value.astype(jnp.bfloat16).astype(jnp.float32)
            both = jnp.concatenate([high, value - high], axis=0).astype(jnp.bfloat16)
            index = where_ref[pl.ds(column(s) * per + row, 1), :]
            table = jnp.where(lanes == jnp.broadcast_to(index, (WIN, WIN)), 1.0, 0.0)
            sums = lax.dot_general(
                both,
                table.astype(jnp.bfloat16),
                (((1,), (1,)), ((), ())),
                preferred_element_type=jnp.float32,
            )
            total = sums[:tall] + sums[tall:]
            sums_ref[column(s), row * (width + 1) : (row + 1) * (width + 1), :] = total[: width + 1]

    def hand_on(s):
        for index in range(members - 1):

            @pl.when(spot == index + 1)
            def _():
                to_chief(s, index).start()

    def add_up(s):
        for index in range(members - 1):
            to_chief(s, index).wait_recv()
        total = sums_ref[column(s)] + pair_ref[0, column(s)]
        for index in range(1, members - 1):
            total = total + pair_ref[index, column(s)]
        pair_ref[0, column(s)] = total

    def step(s, carry):
        deposit(jnp.maximum(s - 1, 0))
        base = column(s) * (per * deep)
        totals = [moved_ref[pl.ds(base + c, per, stride=deep), :] for c in range(comps)]
        for q, value in enumerate(newton(totals, stoich, pairs, logk)):
            species_ref[pl.ds(q, per, stride=tall), :] = value

        @pl.when(s == 1)
        def _():
            @pl.when(spot != 0)
            def _():
                pl.semaphore_wait(barrier, 1)

            @pl.when(jnp.logical_and(spot == 0, target == group))
            def _():
                pl.semaphore_wait(barrier, flow_count - 1)

            @pl.when(jnp.logical_and(spot == 0, target != group))
            def _():
                pl.semaphore_wait(barrier, flow_count)

        @pl.when(s >= 1)
        def _():
            hand_on(s - 1)

        @pl.when(jnp.logical_and(s >= 2, spot == 0))
        def _():
            add_up(s - 2)
            to_owner(s - 2, place).start()

        return carry

    lax.fori_loop(0, flow_count, step, 0)
    last = flow_count - 1
    deposit(last)
    hand_on(last)

    @pl.when(spot == 0)
    def _():
        add_up(last - 1)
        to_owner(last - 1, place).start()
        add_up(last)

        @pl.when(target != group)
        def _():
            to_owner(last, place).start()
            to_owner(last, place).wait_send()

        @pl.when(target == group)
        def _():
            copy = pltpu.make_async_copy(pair_ref.at[0, flow], out_ref.at[place], own_sem)
            copy.start()
            copy.wait()

        for s in range(last):
            to_owner(s, place).wait_send()

    @pl.when(spot != 0)
    def _():
        for s in range(flow_count):
            to_chief(s, 0).wait_send()

    for k in range(share):
        source = sender_flow + k

        @pl.when(jnp.logical_or(source != flow, sender_group != group))
        def _():
            to_owner(0, k).wait_recv()


def react(cells, pick, slot, weight, scale, inflow, stoich, pairs, logk, sizes):
    flow_count, group_count, parts, members, capacity = sizes
    comps = cells.shape[0]
    tiles = pick.shape[0]
    per = capacity // WIN
    width = comps + logk.shape[0]
    deep = -(-comps // 8) * 8
    tall = -(-(width + 1) // 8) * 8
    share = flow_count * parts // group_count
    smem = pl.BlockSpec(memory_space=pltpu.SMEM)
    vmem = pl.BlockSpec(memory_space=pltpu.VMEM)
    chunk = (per * (width + 1), WIN)
    return pl.pallas_call(
        functools.partial(react_kernel, sizes),
        out_shape=jax.ShapeDtypeStruct((share,) + chunk, jnp.float32),
        in_specs=[smem] * 3 + [vmem] * 6,
        out_specs=vmem,
        scratch_shapes=[
            pltpu.VMEM((tiles, WIN), jnp.int32),
            pltpu.VMEM((tiles * deep, WIN), jnp.float32),
            pltpu.VMEM((per * tall, WIN), jnp.float32),
            pltpu.VMEM((flow_count,) + chunk, jnp.float32),
            pltpu.VMEM((members - 1, flow_count) + chunk, jnp.float32),
            pltpu.SemaphoreType.DMA,
            pltpu.SemaphoreType.DMA((flow_count,)),
            pltpu.SemaphoreType.DMA((members - 1, flow_count)),
            pltpu.SemaphoreType.DMA((flow_count,)),
            pltpu.SemaphoreType.DMA((share,)),
        ],
        compiler_params=pltpu.CompilerParams(
            collective_id=1, has_side_effects=True, vmem_limit_bytes=LIMIT
        ),
    )(stoich, pairs, logk, cells, pick, slot, weight, scale, inflow)


def mean_kernel(sums_ref, out_ref):
    width = out_ref.shape[0]
    tall = width + 1
    share, height = sums_ref.shape[:2]
    per = height // tall
    for k in range(share):
        for row in range(per):
            value = sums_ref[k, row * tall : row * tall + width, :]
            count = sums_ref[k, row * tall + width : (row + 1) * tall, :]
            tile = k * per + row
            out_ref[:, tile * WIN : (tile + 1) * WIN] = value / jnp.maximum(count, 1.0)


def mean(sums, width):
    share, height = sums.shape[:2]
    vmem = pl.BlockSpec(memory_space=pltpu.VMEM)
    return pl.pallas_call(
        mean_kernel,
        out_shape=jax.ShapeDtypeStruct((width, share * height // (width + 1) * WIN), jnp.float32),
        in_specs=[vmem],
        out_specs=vmem,
        compiler_params=pltpu.CompilerParams(vmem_limit_bytes=LIMIT),
    )(sums)


def body(cell_state, inflow, courant, pick, node_slot, stoich, logk):
    cell_count = cell_state.shape[1]
    flow_count, group_count = lax.axis_size("flow"), lax.axis_size("group")
    capacity = pick.shape[3]
    parts = cell_count // (flow_count * capacity)
    sizes = (flow_count, group_count, parts, group_count // parts, capacity)
    cells, picks, slots, weight, scale, pairs = forward(
        stoich, cell_state, pick.reshape(flow_count, capacity), node_slot.T, courant.T, sizes
    )
    sums = react(cells, picks, slots, weight, scale, inflow, stoich, pairs, logk, sizes)
    return mean(sums, cell_state.shape[0] + logk.shape[0])


def solution(mesh):
    placed = (
        P(None, "flow"),
        P(None, ("flow", "group")),
        P(None, ("flow", "group")),
        P("group", "flow", None, None),
        P(None, ("flow", "group")),
        P(),
        P(),
    )
    return jax.shard_map(
        body, mesh=mesh, in_specs=placed, out_specs=P(None, ("flow", "group")), check_vma=False
    )
```

```python
import functools

import jax
import jax.numpy as jnp
import numpy as np
from jax import lax
from jax.experimental import pallas as pl
from jax.experimental.pallas import tpu as pltpu
from jax.sharding import PartitionSpec as P

ITERS = 4
WIN = 128
LIMIT = 56 * 1024 * 1024
MESH = pl.DeviceIdType.MESH


def blend(factors, values):
    total = factors[0] * values[0]
    for factor, value in zip(factors[1:], values[1:]):
        total = total + factor * value
    return total


def factor_and_solve(matrix, rhs):
    order = len(rhs)
    lower, inverse, middle = {}, [], []
    for p in range(order):
        for r in range(p + 1):
            total = matrix(p, r)
            for o in range(r):
                total = total - lower[p, o] * lower[r, o]
            if p == r:
                inverse.append(lax.rsqrt(total))
            else:
                lower[p, r] = total * inverse[r]
        total = rhs[p]
        for o in range(p):
            total = total - lower[p, o] * middle[o]
        middle.append(total * inverse[p])
    value = [None] * order
    for p in reversed(range(order)):
        total = middle[p]
        for o in range(p + 1, order):
            total = total - lower[o, p] * value[o]
        value[p] = total * inverse[p]
    return value


def entry(p, r):
    return p * (p + 1) // 2 + r


def spread(comps, plexes):
    first = np.zeros((comps * (comps + 1) // 2 * 8, comps), np.float32)
    second = np.zeros_like(first)
    for p in range(comps):
        for r in range(p + 1):
            first[entry(p, r) * 8 : entry(p, r) * 8 + 8, p] = 1.0
            second[entry(p, r) * 8 : entry(p, r) * 8 + 8, r] = 1.0
    across = np.kron(np.eye(plexes, dtype=np.float32), np.ones((1, 8), np.float32))
    return first, second, across


def newton(totals, stoich, pairs, logk, weights_ref, matrix_ref):
    comps, plexes = len(totals), len(logk)
    columns = [[stoich[p][c] for p in range(plexes)] for c in range(comps)]
    logfree = [jnp.log(t) for t in totals]
    over = [1.0 / t for t in totals]
    backs = [jnp.exp(-(logk[p] + blend(stoich[p], logfree))) for p in range(plexes)]

    def small(p, r):
        total = blend(pairs[p, r], over)
        return total + backs[p] if p == r else total

    value = factor_and_solve(small, [jnp.ones_like(totals[0])] * plexes)
    logfree = [x - o * blend(s, value) for x, o, s in zip(logfree, over, columns)]
    for sweep in range(1, ITERS):
        free = [jnp.exp(x) for x in logfree]
        plex = [jnp.exp(logk[p] + blend(stoich[p], logfree)) for p in range(plexes)]
        stack = jnp.concatenate(plex, axis=0)
        high = stack.astype(jnp.bfloat16)
        low = (stack - high.astype(jnp.float32)).astype(jnp.bfloat16)
        parts = jnp.concatenate([high, high, high, low, low], axis=0)
        matrix_ref[...] = jnp.dot(weights_ref[...], parts, preferred_element_type=jnp.float32)
        rhs = [f + blend(s, plex) - t for f, s, t in zip(free, columns, totals)]

        def full(p, r):
            total = matrix_ref[entry(p, r) * 8 : entry(p, r) * 8 + 8, :]
            return total + free[p] if p == r else total

        update = factor_and_solve(full, rhs)
        logfree = [x - u for x, u in zip(logfree, update)]
    plex = [jnp.exp(logk[p] + blend(stoich[p], logfree)) for p in range(plexes)]
    return [jnp.exp(x) for x in logfree] + plex


def forward_kernel(
    sizes,
    stoich_ref,
    table_s_ref,
    first_ref,
    second_ref,
    across_ref,
    state_ref,
    pick_ref,
    slot_ref,
    courant_ref,
    cells_ref,
    picks_ref,
    slots_ref,
    weight_ref,
    scale_ref,
    pairs_ref,
    weights_ref,
    table_ref,
    turned_ref,
    index_ref,
    own_sem,
    send_sem,
    recv_sem,
    pick_send,
    pick_recv,
):
    flow_count, group_count, parts, members, capacity = sizes
    flow, group = lax.axis_index("flow"), lax.axis_index("group")
    part, rank = lax.rem(group, parts), lax.div(group, parts)
    records = flow_count * capacity
    piece = capacity // members
    others = [
        (flow, lax.rem(rank + m, members) * parts + part) for m in range(1, members)
    ]
    peers = [(lax.rem(flow + d, flow_count), group) for d in range(1, flow_count)]
    barrier = pltpu.get_barrier_semaphore()
    for peer in others + peers:
        pl.semaphore_signal(barrier, inc=1, device_id=peer, device_id_type=MESH)
    per = capacity // WIN
    for k in range(per):
        table_ref[pl.ds(k, flow_count, stride=per), :] = pick_ref[:, k * WIN : (k + 1) * WIN]
    pl.semaphore_wait(barrier, len(others) + len(peers))

    def cut(start, size):
        return pl.ds(pl.multiple_of(start, WIN), size)

    def rows(index):
        return pl.ds(pl.multiple_of(index * per, per), per)

    first = part * records
    for d in range(1, flow_count):
        peer = peers[d - 1]
        pltpu.make_async_remote_copy(
            src_ref=state_ref.at[:, cut(first + peer[0] * capacity + rank * piece, piece)],
            dst_ref=cells_ref.at[:, cut(flow * capacity + rank * piece, piece)],
            send_sem=send_sem.at[0, d],
            recv_sem=recv_sem.at[0, d],
            device_id=peer,
            device_id_type=MESH,
        ).start()
    for d in range(1, flow_count):
        peer = peers[d - 1]
        pltpu.make_async_remote_copy(
            src_ref=table_ref.at[rows(peer[0])],
            dst_ref=picks_ref.at[rows(flow)],
            send_sem=pick_send.at[d],
            recv_sem=pick_recv.at[d],
            device_id=peer,
            device_id_type=MESH,
        ).start()
    mine = [
        pltpu.make_async_copy(
            state_ref.at[:, cut(first + flow * capacity, capacity)],
            cells_ref.at[:, cut(flow * capacity, capacity)],
            own_sem.at[0],
        ),
        pltpu.make_async_copy(table_ref.at[rows(flow)], picks_ref.at[rows(flow)], own_sem.at[1]),
    ]
    for copy in mine:
        copy.start()

    plexes, comps = stoich_ref.shape
    for p in range(plexes):
        for r in range(p + 1):
            for c in range(comps):
                pairs_ref[(p * plexes + r) * comps + c] = stoich_ref[p, c] * stoich_ref[r, c]
    exact = functools.partial(
        lax.dot_general, precision=lax.Precision.HIGHEST, preferred_element_type=jnp.float32
    )
    wide = exact(table_s_ref[...], across_ref[...], (((0,), (0,)), ((), ())))
    products = exact(first_ref[...], wide, (((1,), (0,)), ((), ())))
    products = products * exact(second_ref[...], wide, (((1,), (0,)), ((), ())))
    place = [lax.rem(lax.broadcasted_iota(jnp.int32, products.shape, k), 8) for k in range(2)]
    products = jnp.where(place[0] == place[1], products, 0.0)
    high = products.astype(jnp.bfloat16).astype(jnp.float32)
    rest = products - high
    middle = rest.astype(jnp.bfloat16).astype(jnp.float32)
    split = jnp.concatenate([high, middle, rest - middle, high, middle], axis=1)
    weights_ref[...] = split.astype(jnp.bfloat16)

    tiles = records // WIN
    left = lax.broadcasted_iota(jnp.int32, (tiles, WIN), 1) < WIN // 2

    def by_tile(ref, view):
        value = ref[...]
        view[...] = jnp.transpose(jnp.concatenate([value, value], axis=0))
        even = view[pl.ds(0, tiles, stride=2), :]
        odd = view[pl.ds(1, tiles, stride=2), :]
        return jnp.where(left, even, odd)

    courant = by_tile(courant_ref, turned_ref)
    scale = 1.0 / (1.0 + courant)
    scale_ref[...] = scale
    weight_ref[...] = courant * scale
    slots_ref[...] = by_tile(slot_ref, index_ref) & (WIN - 1)

    def arrival(d, m):
        source = lax.rem(flow + flow_count - d, flow_count)
        owner = lax.rem(rank + members - m, members)
        span = cut(source * capacity + owner * piece, piece)
        return pltpu.make_async_remote_copy(
            src_ref=cells_ref.at[:, span],
            dst_ref=cells_ref.at[:, span],
            send_sem=send_sem.at[m, d],
            recv_sem=recv_sem.at[m, d],
            device_id=others[m - 1] if m else peers[d - 1],
            device_id_type=MESH,
        )

    for d in range(1, flow_count):
        arrival(d, 0).wait_recv()
        source = lax.rem(flow + flow_count - d, flow_count)
        span = cut(source * capacity + rank * piece, piece)
        for m in range(1, members):
            pltpu.make_async_remote_copy(
                src_ref=cells_ref.at[:, span],
                dst_ref=cells_ref.at[:, span],
                send_sem=send_sem.at[m, d],
                recv_sem=recv_sem.at[m, d],
                device_id=others[m - 1],
                device_id_type=MESH,
            ).start()
    for copy in mine:
        copy.wait()
    for d in range(1, flow_count):
        source = lax.rem(flow + flow_count - d, flow_count)
        pltpu.make_async_remote_copy(
            src_ref=table_ref.at[rows(peers[d - 1][0])],
            dst_ref=picks_ref.at[rows(source)],
            send_sem=pick_send.at[d],
            recv_sem=pick_recv.at[d],
            device_id=peers[d - 1],
            device_id_type=MESH,
        ).wait()
        arrival(d, 0).wait_send()
        for m in range(1, members):
            arrival(d, m).wait()


def forward(stoich, state, pick, slot, courant, sizes):
    flow_count, group_count, parts, members, capacity = sizes
    plexes, comps = stoich.shape
    first, second, across = spread(comps, plexes)
    records = flow_count * capacity
    tiles = records // WIN
    anywhere = pl.BlockSpec(memory_space=pl.ANY)
    vmem = pl.BlockSpec(memory_space=pltpu.VMEM)
    smem = pl.BlockSpec(memory_space=pltpu.SMEM)
    table = jax.ShapeDtypeStruct((tiles, WIN), jnp.float32)
    whole = jax.ShapeDtypeStruct((tiles, WIN), jnp.int32)
    return pl.pallas_call(
        functools.partial(forward_kernel, sizes),
        out_shape=(
            jax.ShapeDtypeStruct((comps, records), jnp.float32),
            whole,
            whole,
            table,
            table,
            jax.ShapeDtypeStruct((plexes * plexes * comps,), jnp.float32),
            jax.ShapeDtypeStruct((first.shape[0], 5 * 8 * plexes), jnp.bfloat16),
        ),
        in_specs=[smem, vmem, vmem, vmem, vmem, anywhere, vmem, vmem, vmem],
        out_specs=(vmem, vmem, vmem, vmem, vmem, smem, vmem),
        scratch_shapes=[
            pltpu.VMEM((tiles, WIN), jnp.int32),
            pltpu.VMEM((2 * tiles, WIN), jnp.float32),
            pltpu.VMEM((2 * tiles, WIN), jnp.int32),
            pltpu.SemaphoreType.DMA((2,)),
            pltpu.SemaphoreType.DMA((members, flow_count)),
            pltpu.SemaphoreType.DMA((members, flow_count)),
            pltpu.SemaphoreType.DMA((flow_count,)),
            pltpu.SemaphoreType.DMA((flow_count,)),
        ],
        compiler_params=pltpu.CompilerParams(
            collective_id=0, has_side_effects=True, vmem_limit_bytes=LIMIT
        ),
    )(stoich, stoich, first, second, across, state, pick, slot, courant)


def react_kernel(
    sizes,
    stoich_ref,
    pairs_ref,
    logk_ref,
    cells_ref,
    pick_ref,
    slot_ref,
    weight_ref,
    scale_ref,
    inflow_ref,
    weights_ref,
    out_ref,
    where_ref,
    matrix_ref,
    moved_ref,
    species_ref,
    sums_ref,
    pair_ref,
    own_sem,
    pair_send,
    pair_recv,
    send_sem,
    recv_sem,
):
    flow_count, group_count, parts, members, capacity = sizes
    comps = cells_ref.shape[0]
    plexes = logk_ref.shape[0]
    width = comps + plexes
    tall = species_ref.shape[0] // (capacity // WIN)
    tiles = pick_ref.shape[0]
    per = capacity // WIN
    half = WIN // 2
    deep = moved_ref.shape[0] // tiles

    flow, group = lax.axis_index("flow"), lax.axis_index("group")
    part, rank = lax.rem(group, parts), lax.div(group, parts)
    share = flow_count * parts // group_count

    def chief_of(which):
        return which * members // parts

    chief = chief_of(part)
    spot = lax.rem(rank + members - chief, members)
    target = part * members + lax.div(flow, share)
    sender = lax.div(group, members)
    sender_group = chief_of(sender) * parts + sender
    sender_flow = lax.rem(group, members) * share
    place = lax.rem(flow, share)

    def column(s):
        return lax.rem(flow + 1 + s, flow_count)

    def to_chief(s, index):
        return pltpu.make_async_remote_copy(
            src_ref=sums_ref.at[column(s)],
            dst_ref=pair_ref.at[index, column(s)],
            send_sem=pair_send.at[s],
            recv_sem=pair_recv.at[index, s],
            device_id=(flow, chief * parts + part),
            device_id_type=MESH,
        )

    def to_owner(s, spot_there):
        return pltpu.make_async_remote_copy(
            src_ref=pair_ref.at[0, column(s)],
            dst_ref=out_ref.at[spot_there],
            send_sem=send_sem.at[s],
            recv_sem=recv_sem.at[spot_there],
            device_id=(column(s), target),
            device_id_type=MESH,
        )

    barrier = pltpu.get_barrier_semaphore()
    for k in range(share):
        source = sender_flow + k

        @pl.when(jnp.logical_or(source != flow, sender_group != group))
        def _():
            pl.semaphore_signal(
                barrier, inc=1, device_id=(source, sender_group), device_id_type=MESH
            )

    @pl.when(spot == 0)
    def _():
        for m in range(1, members):
            pl.semaphore_signal(
                barrier,
                inc=1,
                device_id=(flow, lax.rem(chief + m, members) * parts + part),
                device_id_type=MESH,
            )

    where_ref[...] = jnp.take_along_axis(pick_ref[...] & (WIN - 1), slot_ref[...], axis=1)
    left = lax.broadcasted_iota(jnp.int32, (deep, WIN), 1) < half
    zero = jnp.zeros((deep, WIN), jnp.float32)
    inflow = jnp.concatenate([inflow_ref[...], inflow_ref[...]], axis=1)
    inflow = jnp.concatenate([inflow, zero[comps:]], axis=0)

    def transport(t, carry):
        before_w, before_s, moved = carry
        span = pl.ds(pl.multiple_of(t * WIN, WIN), WIN)
        index = jnp.broadcast_to(where_ref[pl.ds(t, 1), :], (deep, WIN))
        block = jnp.concatenate([cells_ref[:, span], zero[comps:]], axis=0)
        old = jnp.take_along_axis(block, index, axis=1)
        weight = jnp.broadcast_to(weight_ref[pl.ds(t, 1), :], (deep, WIN))
        source = old * jnp.broadcast_to(scale_ref[pl.ds(t, 1), :], (deep, WIN))
        turned_w = pltpu.roll(weight, half, 1)
        turned_s = pltpu.roll(source, half, 1)
        both = weight * jnp.where(left, before_w, turned_w)
        added = weight * jnp.where(left, before_s, turned_s) + source
        moved = both * moved + added
        moved_ref[pl.ds(pl.multiple_of(t * deep, deep), deep), :] = moved
        return turned_w, turned_s, moved

    lax.fori_loop(0, tiles, transport, (zero + 1.0, zero, inflow), unroll=8)

    stoich = [[stoich_ref[p, c] for c in range(comps)] for p in range(plexes)]
    logk = [logk_ref[p] for p in range(plexes)]
    pairs = {}
    for p in range(plexes):
        for r in range(p + 1):
            base = (p * plexes + r) * comps
            pairs[p, r] = [pairs_ref[base + c] for c in range(comps)]
    species_ref[...] = jnp.ones_like(species_ref)
    lanes = lax.broadcasted_iota(jnp.int32, (WIN, WIN), 0)

    def deposit(s):
        for row in range(per):
            value = species_ref[row * tall : (row + 1) * tall, :]
            high = value.astype(jnp.bfloat16).astype(jnp.float32)
            both = jnp.concatenate([high, value - high], axis=0).astype(jnp.bfloat16)
            index = where_ref[pl.ds(column(s) * per + row, 1), :]
            table = jnp.where(lanes == jnp.broadcast_to(index, (WIN, WIN)), 1.0, 0.0)
            sums = lax.dot_general(
                both,
                table.astype(jnp.bfloat16),
                (((1,), (1,)), ((), ())),
                preferred_element_type=jnp.float32,
            )
            total = sums[:tall] + sums[tall:]
            sums_ref[column(s), row * (width + 1) : (row + 1) * (width + 1), :] = total[: width + 1]

    def hand_on(s):
        for index in range(members - 1):

            @pl.when(spot == index + 1)
            def _():
                to_chief(s, index).start()

    def add_up(s):
        for index in range(members - 1):
            to_chief(s, index).wait_recv()
        total = sums_ref[column(s)] + pair_ref[0, column(s)]
        for index in range(1, members - 1):
            total = total + pair_ref[index, column(s)]
        pair_ref[0, column(s)] = total

    def step(s, carry):
        deposit(jnp.maximum(s - 1, 0))
        base = column(s) * (per * deep)
        totals = []
        for c in range(comps):
            blocks = [
                moved_ref[pl.ds(base + 8 * k * deep + c, 8, stride=deep), :]
                for k in range(per // 8)
            ]
            totals.append(jnp.concatenate(blocks, axis=1))
        species = newton(totals, stoich, pairs, logk, weights_ref, matrix_ref)
        for q, value in enumerate(species):
            for k in range(per // 8):
                species_ref[pl.ds(8 * k * tall + q, 8, stride=tall), :] = value[
                    :, k * WIN : (k + 1) * WIN
                ]

        @pl.when(s == 1)
        def _():
            @pl.when(spot != 0)
            def _():
                pl.semaphore_wait(barrier, 1)

            @pl.when(jnp.logical_and(spot == 0, target == group))
            def _():
                pl.semaphore_wait(barrier, flow_count - 1)

            @pl.when(jnp.logical_and(spot == 0, target != group))
            def _():
                pl.semaphore_wait(barrier, flow_count)

        @pl.when(s >= 1)
        def _():
            hand_on(s - 1)

        @pl.when(jnp.logical_and(s >= 2, spot == 0))
        def _():
            add_up(s - 2)
            to_owner(s - 2, place).start()

        return carry

    lax.fori_loop(0, flow_count, step, 0)
    last = flow_count - 1
    deposit(last)
    hand_on(last)

    @pl.when(spot == 0)
    def _():
        add_up(last - 1)
        to_owner(last - 1, place).start()
        add_up(last)

        @pl.when(target != group)
        def _():
            to_owner(last, place).start()
            to_owner(last, place).wait_send()

        @pl.when(target == group)
        def _():
            copy = pltpu.make_async_copy(pair_ref.at[0, flow], out_ref.at[place], own_sem)
            copy.start()
            copy.wait()

        for s in range(last):
            to_owner(s, place).wait_send()

    @pl.when(spot != 0)
    def _():
        for s in range(flow_count):
            to_chief(s, 0).wait_send()

    for k in range(share):
        source = sender_flow + k

        @pl.when(jnp.logical_or(source != flow, sender_group != group))
        def _():
            to_owner(0, k).wait_recv()


def react(cells, pick, slot, weight, scale, inflow, weights, stoich, pairs, logk, sizes):
    flow_count, group_count, parts, members, capacity = sizes
    comps = cells.shape[0]
    tiles = pick.shape[0]
    per = capacity // WIN
    width = comps + logk.shape[0]
    deep = -(-comps // 8) * 8
    tall = -(-(width + 1) // 8) * 8
    share = flow_count * parts // group_count
    smem = pl.BlockSpec(memory_space=pltpu.SMEM)
    vmem = pl.BlockSpec(memory_space=pltpu.VMEM)
    chunk = (per * (width + 1), WIN)
    return pl.pallas_call(
        functools.partial(react_kernel, sizes),
        out_shape=jax.ShapeDtypeStruct((share,) + chunk, jnp.float32),
        in_specs=[smem] * 3 + [vmem] * 7,
        out_specs=vmem,
        scratch_shapes=[
            pltpu.VMEM((tiles, WIN), jnp.int32),
            pltpu.VMEM((weights.shape[0], per * WIN // 8), jnp.float32),
            pltpu.VMEM((tiles * deep, WIN), jnp.float32),
            pltpu.VMEM((per * tall, WIN), jnp.float32),
            pltpu.VMEM((flow_count,) + chunk, jnp.float32),
            pltpu.VMEM((members - 1, flow_count) + chunk, jnp.float32),
            pltpu.SemaphoreType.DMA,
            pltpu.SemaphoreType.DMA((flow_count,)),
            pltpu.SemaphoreType.DMA((members - 1, flow_count)),
            pltpu.SemaphoreType.DMA((flow_count,)),
            pltpu.SemaphoreType.DMA((share,)),
        ],
        compiler_params=pltpu.CompilerParams(
            collective_id=1, has_side_effects=True, vmem_limit_bytes=LIMIT
        ),
    )(stoich, pairs, logk, cells, pick, slot, weight, scale, inflow, weights)


def mean_kernel(sums_ref, out_ref):
    width = out_ref.shape[0]
    tall = width + 1
    for row in range(sums_ref.shape[1] // tall):
        value = sums_ref[0, row * tall : row * tall + width, :]
        count = sums_ref[0, row * tall + width : (row + 1) * tall, :]
        out_ref[:, row * WIN : (row + 1) * WIN] = value / jnp.maximum(count, 1.0)


def mean(sums, width):
    share, height = sums.shape[:2]
    columns = height // (width + 1) * WIN
    return pl.pallas_call(
        mean_kernel,
        out_shape=jax.ShapeDtypeStruct((width, share * columns), jnp.float32),
        grid=(share,),
        in_specs=[pl.BlockSpec((1, height, WIN), lambda k: (k, 0, 0))],
        out_specs=pl.BlockSpec((width, columns), lambda k: (0, k)),
        compiler_params=pltpu.CompilerParams(vmem_limit_bytes=LIMIT),
    )(sums)


def body(cell_state, inflow, courant, pick, node_slot, stoich, logk):
    cell_count = cell_state.shape[1]
    flow_count, group_count = lax.axis_size("flow"), lax.axis_size("group")
    capacity = pick.shape[3]
    parts = cell_count // (flow_count * capacity)
    sizes = (flow_count, group_count, parts, group_count // parts, capacity)
    cells, picks, slots, weight, scale, pairs, weights = forward(
        stoich, cell_state, pick.reshape(flow_count, capacity), node_slot.T, courant.T, sizes
    )
    sums = react(cells, picks, slots, weight, scale, inflow, weights, stoich, pairs, logk, sizes)
    return mean(sums, cell_state.shape[0] + logk.shape[0])


def solution(mesh):
    placed = (
        P(None, "flow"),
        P(None, ("flow", "group")),
        P(None, ("flow", "group")),
        P("group", "flow", None, None),
        P(None, ("flow", "group")),
        P(),
        P(),
    )
    return jax.shard_map(
        body, mesh=mesh, in_specs=placed, out_specs=P(None, ("flow", "group")), check_vma=False
    )
```

```python
import functools

import jax
import jax.numpy as jnp
import numpy as np
from jax import lax
from jax.experimental import pallas as pl
from jax.experimental.pallas import tpu as pltpu
from jax.sharding import PartitionSpec as P

ITERS = 4
WIN = 128
LIMIT = 56 * 1024 * 1024
MESH = pl.DeviceIdType.MESH


def blend(factors, values):
    total = factors[0] * values[0]
    for factor, value in zip(factors[1:], values[1:]):
        total = total + factor * value
    return total


def factor_and_solve(matrix, rhs):
    order = len(rhs)
    lower, inverse, middle = {}, [], []
    for p in range(order):
        for r in range(p + 1):
            total = matrix(p, r)
            for o in range(r):
                total = total - lower[p, o] * lower[r, o]
            if p == r:
                inverse.append(lax.rsqrt(total))
            else:
                lower[p, r] = total * inverse[r]
        total = rhs[p]
        for o in range(p):
            total = total - lower[p, o] * middle[o]
        middle.append(total * inverse[p])
    value = [None] * order
    for p in reversed(range(order)):
        total = middle[p]
        for o in range(p + 1, order):
            total = total - lower[o, p] * value[o]
        value[p] = total * inverse[p]
    return value


def entry(p, r):
    return p * (p + 1) // 2 + r


def spread(comps, plexes):
    first = np.zeros((comps * (comps + 1) // 2 * 8, comps), np.float32)
    second = np.zeros_like(first)
    for p in range(comps):
        for r in range(p + 1):
            first[entry(p, r) * 8 : entry(p, r) * 8 + 8, p] = 1.0
            second[entry(p, r) * 8 : entry(p, r) * 8 + 8, r] = 1.0
    across = np.kron(np.eye(plexes, dtype=np.float32), np.ones((1, 8), np.float32))
    return first, second, across


def newton(totals, stoich, pairs, logk, weights_ref, matrix_ref):
    comps, plexes = len(totals), len(logk)
    columns = [[stoich[p][c] for p in range(plexes)] for c in range(comps)]
    logfree = [jnp.log(t) for t in totals]
    over = [1.0 / t for t in totals]
    backs = [jnp.exp(-(logk[p] + blend(stoich[p], logfree))) for p in range(plexes)]

    def small(p, r):
        total = blend(pairs[p, r], over)
        return total + backs[p] if p == r else total

    value = factor_and_solve(small, [jnp.ones_like(totals[0])] * plexes)
    logfree = [x - o * blend(s, value) for x, o, s in zip(logfree, over, columns)]
    for sweep in range(1, ITERS):
        free = [jnp.exp(x) for x in logfree]
        plex = [jnp.exp(logk[p] + blend(stoich[p], logfree)) for p in range(plexes)]
        stack = jnp.concatenate(plex, axis=0)
        high = stack.astype(jnp.bfloat16)
        low = (stack - high.astype(jnp.float32)).astype(jnp.bfloat16)
        parts = jnp.concatenate([high, high, high, low, low], axis=0)
        matrix_ref[...] = jnp.dot(weights_ref[...], parts, preferred_element_type=jnp.float32)
        rhs = [f + blend(s, plex) - t for f, s, t in zip(free, columns, totals)]

        def full(p, r):
            total = matrix_ref[entry(p, r) * 8 : entry(p, r) * 8 + 8, :]
            return total + free[p] if p == r else total

        update = factor_and_solve(full, rhs)
        logfree = [x - u for x, u in zip(logfree, update)]
    plex = [jnp.exp(logk[p] + blend(stoich[p], logfree)) for p in range(plexes)]
    return [jnp.exp(x) for x in logfree] + plex


def forward_kernel(
    sizes,
    stoich_ref,
    table_s_ref,
    first_ref,
    second_ref,
    across_ref,
    state_ref,
    pick_ref,
    slot_ref,
    courant_ref,
    cells_ref,
    picks_ref,
    slots_ref,
    weight_ref,
    scale_ref,
    pairs_ref,
    weights_ref,
    table_ref,
    turned_ref,
    index_ref,
    own_sem,
    send_sem,
    recv_sem,
    pick_send,
    pick_recv,
):
    flow_count, group_count, parts, members, capacity = sizes
    flow, group = lax.axis_index("flow"), lax.axis_index("group")
    part, rank = lax.rem(group, parts), lax.div(group, parts)
    records = flow_count * capacity
    piece = capacity // members
    others = [
        (flow, lax.rem(rank + m, members) * parts + part) for m in range(1, members)
    ]
    peers = [(lax.rem(flow + d, flow_count), group) for d in range(1, flow_count)]
    barrier = pltpu.get_barrier_semaphore()
    for peer in others + peers:
        pl.semaphore_signal(barrier, inc=1, device_id=peer, device_id_type=MESH)
    per = capacity // WIN
    for k in range(per):
        table_ref[pl.ds(k, flow_count, stride=per), :] = pick_ref[:, k * WIN : (k + 1) * WIN]
    pl.semaphore_wait(barrier, len(others) + len(peers))

    def cut(start, size):
        return pl.ds(pl.multiple_of(start, WIN), size)

    def rows(index):
        return pl.ds(pl.multiple_of(index * per, per), per)

    first = part * records
    for d in range(1, flow_count):
        peer = peers[d - 1]
        pltpu.make_async_remote_copy(
            src_ref=state_ref.at[:, cut(first + peer[0] * capacity + rank * piece, piece)],
            dst_ref=cells_ref.at[:, cut(flow * capacity + rank * piece, piece)],
            send_sem=send_sem.at[0, d],
            recv_sem=recv_sem.at[0, d],
            device_id=peer,
            device_id_type=MESH,
        ).start()
    for d in range(1, flow_count):
        peer = peers[d - 1]
        pltpu.make_async_remote_copy(
            src_ref=table_ref.at[rows(peer[0])],
            dst_ref=picks_ref.at[rows(flow)],
            send_sem=pick_send.at[d],
            recv_sem=pick_recv.at[d],
            device_id=peer,
            device_id_type=MESH,
        ).start()
    mine = [
        pltpu.make_async_copy(
            state_ref.at[:, cut(first + flow * capacity, capacity)],
            cells_ref.at[:, cut(flow * capacity, capacity)],
            own_sem.at[0],
        ),
        pltpu.make_async_copy(table_ref.at[rows(flow)], picks_ref.at[rows(flow)], own_sem.at[1]),
    ]
    for copy in mine:
        copy.start()

    plexes, comps = stoich_ref.shape
    for p in range(plexes):
        for r in range(p + 1):
            for c in range(comps):
                pairs_ref[(p * plexes + r) * comps + c] = stoich_ref[p, c] * stoich_ref[r, c]
    exact = functools.partial(
        lax.dot_general, precision=lax.Precision.HIGHEST, preferred_element_type=jnp.float32
    )
    wide = exact(table_s_ref[...], across_ref[...], (((0,), (0,)), ((), ())))
    products = exact(first_ref[...], wide, (((1,), (0,)), ((), ())))
    products = products * exact(second_ref[...], wide, (((1,), (0,)), ((), ())))
    place = [lax.rem(lax.broadcasted_iota(jnp.int32, products.shape, k), 8) for k in range(2)]
    products = jnp.where(place[0] == place[1], products, 0.0)
    high = products.astype(jnp.bfloat16).astype(jnp.float32)
    rest = products - high
    middle = rest.astype(jnp.bfloat16).astype(jnp.float32)
    split = jnp.concatenate([high, middle, rest - middle, high, middle], axis=1)
    weights_ref[...] = split.astype(jnp.bfloat16)

    tiles = records // WIN
    left = lax.broadcasted_iota(jnp.int32, (tiles, WIN), 1) < WIN // 2

    def by_tile(ref, view):
        value = ref[...]
        view[...] = jnp.transpose(jnp.concatenate([value, value], axis=0))
        even = view[pl.ds(0, tiles, stride=2), :]
        odd = view[pl.ds(1, tiles, stride=2), :]
        return jnp.where(left, even, odd)

    courant = by_tile(courant_ref, turned_ref)
    scale = 1.0 / (1.0 + courant)
    scale_ref[...] = scale
    weight_ref[...] = courant * scale
    slots_ref[...] = by_tile(slot_ref, index_ref) & (WIN - 1)

    def arrival(d, m):
        source = lax.rem(flow + flow_count - d, flow_count)
        owner = lax.rem(rank + members - m, members)
        span = cut(source * capacity + owner * piece, piece)
        return pltpu.make_async_remote_copy(
            src_ref=cells_ref.at[:, span],
            dst_ref=cells_ref.at[:, span],
            send_sem=send_sem.at[m, d],
            recv_sem=recv_sem.at[m, d],
            device_id=others[m - 1] if m else peers[d - 1],
            device_id_type=MESH,
        )

    for d in range(1, flow_count):
        arrival(d, 0).wait_recv()
        source = lax.rem(flow + flow_count - d, flow_count)
        span = cut(source * capacity + rank * piece, piece)
        for m in range(1, members):
            pltpu.make_async_remote_copy(
                src_ref=cells_ref.at[:, span],
                dst_ref=cells_ref.at[:, span],
                send_sem=send_sem.at[m, d],
                recv_sem=recv_sem.at[m, d],
                device_id=others[m - 1],
                device_id_type=MESH,
            ).start()
    for copy in mine:
        copy.wait()
    for d in range(1, flow_count):
        source = lax.rem(flow + flow_count - d, flow_count)
        pltpu.make_async_remote_copy(
            src_ref=table_ref.at[rows(peers[d - 1][0])],
            dst_ref=picks_ref.at[rows(source)],
            send_sem=pick_send.at[d],
            recv_sem=pick_recv.at[d],
            device_id=peers[d - 1],
            device_id_type=MESH,
        ).wait()
        arrival(d, 0).wait_send()
        for m in range(1, members):
            arrival(d, m).wait()


def forward(stoich, state, pick, slot, courant, sizes):
    flow_count, group_count, parts, members, capacity = sizes
    plexes, comps = stoich.shape
    first, second, across = spread(comps, plexes)
    records = flow_count * capacity
    tiles = records // WIN
    anywhere = pl.BlockSpec(memory_space=pl.ANY)
    vmem = pl.BlockSpec(memory_space=pltpu.VMEM)
    smem = pl.BlockSpec(memory_space=pltpu.SMEM)
    table = jax.ShapeDtypeStruct((tiles, WIN), jnp.float32)
    whole = jax.ShapeDtypeStruct((tiles, WIN), jnp.int32)
    return pl.pallas_call(
        functools.partial(forward_kernel, sizes),
        out_shape=(
            jax.ShapeDtypeStruct((comps, records), jnp.float32),
            whole,
            whole,
            table,
            table,
            jax.ShapeDtypeStruct((plexes * plexes * comps,), jnp.float32),
            jax.ShapeDtypeStruct((first.shape[0], 5 * 8 * plexes), jnp.bfloat16),
        ),
        in_specs=[smem, vmem, vmem, vmem, vmem, anywhere, vmem, vmem, vmem],
        out_specs=(vmem, vmem, vmem, vmem, vmem, smem, vmem),
        scratch_shapes=[
            pltpu.VMEM((tiles, WIN), jnp.int32),
            pltpu.VMEM((2 * tiles, WIN), jnp.float32),
            pltpu.VMEM((2 * tiles, WIN), jnp.int32),
            pltpu.SemaphoreType.DMA((2,)),
            pltpu.SemaphoreType.DMA((members, flow_count)),
            pltpu.SemaphoreType.DMA((members, flow_count)),
            pltpu.SemaphoreType.DMA((flow_count,)),
            pltpu.SemaphoreType.DMA((flow_count,)),
        ],
        compiler_params=pltpu.CompilerParams(
            collective_id=0, has_side_effects=True, vmem_limit_bytes=LIMIT
        ),
    )(stoich, stoich, first, second, across, state, pick, slot, courant)


def react_kernel(
    sizes,
    stoich_ref,
    pairs_ref,
    logk_ref,
    cells_ref,
    pick_ref,
    slot_ref,
    weight_ref,
    scale_ref,
    inflow_ref,
    weights_ref,
    out_ref,
    where_ref,
    matrix_ref,
    moved_ref,
    species_ref,
    sums_ref,
    pair_ref,
    own_sem,
    pair_send,
    pair_recv,
    send_sem,
    recv_sem,
):
    flow_count, group_count, parts, members, capacity = sizes
    comps = cells_ref.shape[0]
    plexes = logk_ref.shape[0]
    width = comps + plexes
    tall = species_ref.shape[0] // (capacity // WIN)
    tiles = pick_ref.shape[0]
    per = capacity // WIN
    half = WIN // 2
    deep = moved_ref.shape[0] // tiles

    flow, group = lax.axis_index("flow"), lax.axis_index("group")
    part, rank = lax.rem(group, parts), lax.div(group, parts)
    share = flow_count * parts // group_count

    def chief_of(which):
        return which * members // parts

    chief = chief_of(part)
    spot = lax.rem(rank + members - chief, members)
    target = part * members + lax.div(flow, share)
    sender = lax.div(group, members)
    sender_group = chief_of(sender) * parts + sender
    sender_flow = lax.rem(group, members) * share
    place = lax.rem(flow, share)

    def column(s):
        return lax.rem(flow + 1 + s, flow_count)

    def to_chief(s, index):
        return pltpu.make_async_remote_copy(
            src_ref=sums_ref.at[column(s)],
            dst_ref=pair_ref.at[index, column(s)],
            send_sem=pair_send.at[s],
            recv_sem=pair_recv.at[index, s],
            device_id=(flow, chief * parts + part),
            device_id_type=MESH,
        )

    def to_owner(s, spot_there):
        return pltpu.make_async_remote_copy(
            src_ref=pair_ref.at[0, column(s)],
            dst_ref=out_ref.at[spot_there],
            send_sem=send_sem.at[s],
            recv_sem=recv_sem.at[spot_there],
            device_id=(column(s), target),
            device_id_type=MESH,
        )

    barrier = pltpu.get_barrier_semaphore()
    for k in range(share):
        source = sender_flow + k

        @pl.when(jnp.logical_or(source != flow, sender_group != group))
        def _():
            pl.semaphore_signal(
                barrier, inc=1, device_id=(source, sender_group), device_id_type=MESH
            )

    @pl.when(spot == 0)
    def _():
        for m in range(1, members):
            pl.semaphore_signal(
                barrier,
                inc=1,
                device_id=(flow, lax.rem(chief + m, members) * parts + part),
                device_id_type=MESH,
            )

    where_ref[...] = jnp.take_along_axis(pick_ref[...] & (WIN - 1), slot_ref[...], axis=1)
    left = lax.broadcasted_iota(jnp.int32, (deep, WIN), 1) < half
    zero = jnp.zeros((deep, WIN), jnp.float32)
    inflow = jnp.concatenate([inflow_ref[...], inflow_ref[...]], axis=1)
    inflow = jnp.concatenate([inflow, zero[comps:]], axis=0)

    def transport(t, carry):
        before_w, before_s, moved = carry
        span = pl.ds(pl.multiple_of(t * WIN, WIN), WIN)
        index = jnp.broadcast_to(where_ref[pl.ds(t, 1), :], (deep, WIN))
        block = jnp.concatenate([cells_ref[:, span], zero[comps:]], axis=0)
        old = jnp.take_along_axis(block, index, axis=1)
        weight = jnp.broadcast_to(weight_ref[pl.ds(t, 1), :], (deep, WIN))
        source = old * jnp.broadcast_to(scale_ref[pl.ds(t, 1), :], (deep, WIN))
        turned_w = pltpu.roll(weight, half, 1)
        turned_s = pltpu.roll(source, half, 1)
        both = weight * jnp.where(left, before_w, turned_w)
        added = weight * jnp.where(left, before_s, turned_s) + source
        moved = both * moved + added
        moved_ref[pl.ds(pl.multiple_of(t * deep, deep), deep), :] = moved
        return turned_w, turned_s, moved

    lax.fori_loop(0, tiles, transport, (zero + 1.0, zero, inflow), unroll=8)

    stoich = [[stoich_ref[p, c] for c in range(comps)] for p in range(plexes)]
    logk = [logk_ref[p] for p in range(plexes)]
    pairs = {}
    for p in range(plexes):
        for r in range(p + 1):
            base = (p * plexes + r) * comps
            pairs[p, r] = [pairs_ref[base + c] for c in range(comps)]
    species_ref[...] = jnp.ones_like(species_ref)
    lanes = lax.broadcasted_iota(jnp.int32, (WIN, WIN), 0)

    def deposit(s):
        for row in range(per):
            value = species_ref[row * tall : (row + 1) * tall, :]
            high = value.astype(jnp.bfloat16).astype(jnp.float32)
            both = jnp.concatenate([high, value - high], axis=0).astype(jnp.bfloat16)
            index = where_ref[pl.ds(column(s) * per + row, 1), :]
            table = jnp.where(lanes == jnp.broadcast_to(index, (WIN, WIN)), 1.0, 0.0)
            sums = lax.dot_general(
                both,
                table.astype(jnp.bfloat16),
                (((1,), (1,)), ((), ())),
                preferred_element_type=jnp.float32,
            )
            total = sums[:tall] + sums[tall:]
            sums_ref[column(s), row * (width + 1) : (row + 1) * (width + 1), :] = total[: width + 1]

    def hand_on(s):
        for index in range(members - 1):

            @pl.when(spot == index + 1)
            def _():
                to_chief(s, index).start()

    def add_up(s):
        for index in range(members - 1):
            to_chief(s, index).wait_recv()
        total = sums_ref[column(s)] + pair_ref[0, column(s)]
        for index in range(1, members - 1):
            total = total + pair_ref[index, column(s)]
        pair_ref[0, column(s)] = total

    def step(s, carry):
        deposit(jnp.maximum(s - 1, 0))

        @pl.when(s == 1)
        def _():
            @pl.when(spot != 0)
            def _():
                pl.semaphore_wait(barrier, 1)

            @pl.when(jnp.logical_and(spot == 0, target == group))
            def _():
                pl.semaphore_wait(barrier, flow_count - 1)

            @pl.when(jnp.logical_and(spot == 0, target != group))
            def _():
                pl.semaphore_wait(barrier, flow_count)

        @pl.when(s >= 1)
        def _():
            hand_on(s - 1)

        base = column(s) * (per * deep)
        totals = []
        for c in range(comps):
            blocks = [
                moved_ref[pl.ds(base + 8 * k * deep + c, 8, stride=deep), :]
                for k in range(per // 8)
            ]
            totals.append(jnp.concatenate(blocks, axis=1))
        species = newton(totals, stoich, pairs, logk, weights_ref, matrix_ref)
        for q, value in enumerate(species):
            for k in range(per // 8):
                species_ref[pl.ds(8 * k * tall + q, 8, stride=tall), :] = value[
                    :, k * WIN : (k + 1) * WIN
                ]

        @pl.when(jnp.logical_and(s >= 1, spot == 0))
        def _():
            add_up(s - 1)
            to_owner(s - 1, place).start()

        return carry

    lax.fori_loop(0, flow_count, step, 0)
    last = flow_count - 1
    deposit(last)
    hand_on(last)

    @pl.when(spot == 0)
    def _():
        add_up(last)

        @pl.when(target != group)
        def _():
            to_owner(last, place).start()
            to_owner(last, place).wait_send()

        @pl.when(target == group)
        def _():
            copy = pltpu.make_async_copy(pair_ref.at[0, flow], out_ref.at[place], own_sem)
            copy.start()
            copy.wait()

        for s in range(last):
            to_owner(s, place).wait_send()

    @pl.when(spot != 0)
    def _():
        for s in range(flow_count):
            to_chief(s, 0).wait_send()

    for k in range(share):
        source = sender_flow + k

        @pl.when(jnp.logical_or(source != flow, sender_group != group))
        def _():
            to_owner(0, k).wait_recv()


def react(cells, pick, slot, weight, scale, inflow, weights, stoich, pairs, logk, sizes):
    flow_count, group_count, parts, members, capacity = sizes
    comps = cells.shape[0]
    tiles = pick.shape[0]
    per = capacity // WIN
    width = comps + logk.shape[0]
    deep = -(-comps // 8) * 8
    tall = -(-(width + 1) // 8) * 8
    share = flow_count * parts // group_count
    smem = pl.BlockSpec(memory_space=pltpu.SMEM)
    vmem = pl.BlockSpec(memory_space=pltpu.VMEM)
    chunk = (per * (width + 1), WIN)
    return pl.pallas_call(
        functools.partial(react_kernel, sizes),
        out_shape=jax.ShapeDtypeStruct((share,) + chunk, jnp.float32),
        in_specs=[smem] * 3 + [vmem] * 7,
        out_specs=vmem,
        scratch_shapes=[
            pltpu.VMEM((tiles, WIN), jnp.int32),
            pltpu.VMEM((weights.shape[0], per * WIN // 8), jnp.float32),
            pltpu.VMEM((tiles * deep, WIN), jnp.float32),
            pltpu.VMEM((per * tall, WIN), jnp.float32),
            pltpu.VMEM((flow_count,) + chunk, jnp.float32),
            pltpu.VMEM((members - 1, flow_count) + chunk, jnp.float32),
            pltpu.SemaphoreType.DMA,
            pltpu.SemaphoreType.DMA((flow_count,)),
            pltpu.SemaphoreType.DMA((members - 1, flow_count)),
            pltpu.SemaphoreType.DMA((flow_count,)),
            pltpu.SemaphoreType.DMA((share,)),
        ],
        compiler_params=pltpu.CompilerParams(
            collective_id=1, has_side_effects=True, vmem_limit_bytes=LIMIT
        ),
    )(stoich, pairs, logk, cells, pick, slot, weight, scale, inflow, weights)


def mean_kernel(sums_ref, out_ref):
    width = out_ref.shape[0]
    tall = width + 1
    share, height = sums_ref.shape[:2]
    per = height // tall
    for k in range(share):
        for row in range(per):
            value = sums_ref[k, row * tall : row * tall + width, :]
            count = sums_ref[k, row * tall + width : (row + 1) * tall, :]
            tile = k * per + row
            out_ref[:, tile * WIN : (tile + 1) * WIN] = value * (1.0 / jnp.maximum(count, 1.0))


def mean(sums, width):
    share, height = sums.shape[:2]
    vmem = pl.BlockSpec(memory_space=pltpu.VMEM)
    return pl.pallas_call(
        mean_kernel,
        out_shape=jax.ShapeDtypeStruct((width, share * height // (width + 1) * WIN), jnp.float32),
        in_specs=[vmem],
        out_specs=vmem,
        compiler_params=pltpu.CompilerParams(vmem_limit_bytes=LIMIT),
    )(sums)


def body(cell_state, inflow, courant, pick, node_slot, stoich, logk):
    cell_count = cell_state.shape[1]
    flow_count, group_count = lax.axis_size("flow"), lax.axis_size("group")
    capacity = pick.shape[3]
    parts = cell_count // (flow_count * capacity)
    sizes = (flow_count, group_count, parts, group_count // parts, capacity)
    cells, picks, slots, weight, scale, pairs, weights = forward(
        stoich, cell_state, pick.reshape(flow_count, capacity), node_slot.T, courant.T, sizes
    )
    sums = react(cells, picks, slots, weight, scale, inflow, weights, stoich, pairs, logk, sizes)
    return mean(sums, cell_state.shape[0] + logk.shape[0])


def solution(mesh):
    placed = (
        P(None, "flow"),
        P(None, ("flow", "group")),
        P(None, ("flow", "group")),
        P("group", "flow", None, None),
        P(None, ("flow", "group")),
        P(),
        P(),
    )
    return jax.shard_map(
        body, mesh=mesh, in_specs=placed, out_specs=P(None, ("flow", "group")), check_vma=False
    )
```

```python
import functools

import jax
import jax.numpy as jnp
import numpy as np
from jax import lax
from jax.experimental import pallas as pl
from jax.experimental.pallas import tpu as pltpu
from jax.sharding import PartitionSpec as P

ITERS = 4
WIN = 128
LIMIT = 56 * 1024 * 1024
MESH = pl.DeviceIdType.MESH


def blend(factors, values):
    total = factors[0] * values[0]
    for factor, value in zip(factors[1:], values[1:]):
        total = total + factor * value
    return total


def factor_and_solve(matrix, rhs):
    order = len(rhs)
    lower, inverse, middle = {}, [], []
    for p in range(order):
        for r in range(p + 1):
            total = matrix(p, r)
            for o in range(r):
                total = total - lower[p, o] * lower[r, o]
            if p == r:
                inverse.append(lax.rsqrt(total))
            else:
                lower[p, r] = total * inverse[r]
        total = rhs[p]
        for o in range(p):
            total = total - lower[p, o] * middle[o]
        middle.append(total * inverse[p])
    value = [None] * order
    for p in reversed(range(order)):
        total = middle[p]
        for o in range(p + 1, order):
            total = total - lower[o, p] * value[o]
        value[p] = total * inverse[p]
    return value


def entry(p, r):
    return p * (p + 1) // 2 + r


def spread(comps, plexes):
    first = np.zeros((comps * (comps + 1) // 2 * 8, comps), np.float32)
    second = np.zeros_like(first)
    for p in range(comps):
        for r in range(p + 1):
            first[entry(p, r) * 8 : entry(p, r) * 8 + 8, p] = 1.0
            second[entry(p, r) * 8 : entry(p, r) * 8 + 8, r] = 1.0
    across = np.kron(np.eye(plexes, dtype=np.float32), np.ones((1, 8), np.float32))
    return first, second, across


def newton(totals, stoich, pairs, logk, weights_ref, matrix_ref):
    comps, plexes = len(totals), len(logk)
    columns = [[stoich[p][c] for p in range(plexes)] for c in range(comps)]
    logfree = [jnp.log(t) for t in totals]
    over = [1.0 / t for t in totals]
    backs = [jnp.exp(-(logk[p] + blend(stoich[p], logfree))) for p in range(plexes)]

    def small(p, r):
        total = blend(pairs[p, r], over)
        return total + backs[p] if p == r else total

    value = factor_and_solve(small, [jnp.ones_like(totals[0])] * plexes)
    logfree = [x - o * blend(s, value) for x, o, s in zip(logfree, over, columns)]
    for sweep in range(1, ITERS):
        free = [jnp.exp(x) for x in logfree]
        plex = [jnp.exp(logk[p] + blend(stoich[p], logfree)) for p in range(plexes)]
        stack = jnp.concatenate(plex, axis=0)
        high = stack.astype(jnp.bfloat16)
        low = (stack - high.astype(jnp.float32)).astype(jnp.bfloat16)
        parts = jnp.concatenate([high, high, high, low, low], axis=0)
        matrix_ref[...] = jnp.dot(weights_ref[...], parts, preferred_element_type=jnp.float32)
        rhs = [f + blend(s, plex) - t for f, s, t in zip(free, columns, totals)]

        def full(p, r):
            total = matrix_ref[entry(p, r) * 8 : entry(p, r) * 8 + 8, :]
            return total + free[p] if p == r else total

        update = factor_and_solve(full, rhs)
        logfree = [x - u for x, u in zip(logfree, update)]
    plex = [jnp.exp(logk[p] + blend(stoich[p], logfree)) for p in range(plexes)]
    return [jnp.exp(x) for x in logfree] + plex


def forward_kernel(
    sizes,
    stoich_ref,
    table_s_ref,
    first_ref,
    second_ref,
    across_ref,
    state_ref,
    pick_ref,
    slot_ref,
    courant_ref,
    cells_ref,
    picks_ref,
    slots_ref,
    weight_ref,
    scale_ref,
    pairs_ref,
    weights_ref,
    table_ref,
    turned_ref,
    index_ref,
    own_sem,
    send_sem,
    recv_sem,
    pick_send,
    pick_recv,
):
    flow_count, group_count, parts, members, capacity = sizes
    flow, group = lax.axis_index("flow"), lax.axis_index("group")
    part, rank = lax.rem(group, parts), lax.div(group, parts)
    records = flow_count * capacity
    piece = capacity // members
    others = [
        (flow, lax.rem(rank + m, members) * parts + part) for m in range(1, members)
    ]
    peers = [(lax.rem(flow + d, flow_count), group) for d in range(1, flow_count)]
    barrier = pltpu.get_barrier_semaphore()
    for peer in others + peers:
        pl.semaphore_signal(barrier, inc=1, device_id=peer, device_id_type=MESH)
    per = capacity // WIN
    for k in range(per):
        table_ref[pl.ds(k, flow_count, stride=per), :] = pick_ref[:, k * WIN : (k + 1) * WIN]
    pl.semaphore_wait(barrier, len(others) + len(peers))

    def cut(start, size):
        return pl.ds(pl.multiple_of(start, WIN), size)

    def rows(index):
        return pl.ds(pl.multiple_of(index * per, per), per)

    first = part * records
    for d in range(1, flow_count):
        peer = peers[d - 1]
        pltpu.make_async_remote_copy(
            src_ref=state_ref.at[:, cut(first + peer[0] * capacity + rank * piece, piece)],
            dst_ref=cells_ref.at[:, cut(flow * capacity + rank * piece, piece)],
            send_sem=send_sem.at[0, d],
            recv_sem=recv_sem.at[0, d],
            device_id=peer,
            device_id_type=MESH,
        ).start()
    for d in range(1, flow_count):
        peer = peers[d - 1]
        pltpu.make_async_remote_copy(
            src_ref=table_ref.at[rows(peer[0])],
            dst_ref=picks_ref.at[rows(flow)],
            send_sem=pick_send.at[d],
            recv_sem=pick_recv.at[d],
            device_id=peer,
            device_id_type=MESH,
        ).start()
    mine = [
        pltpu.make_async_copy(
            state_ref.at[:, cut(first + flow * capacity, capacity)],
            cells_ref.at[:, cut(flow * capacity, capacity)],
            own_sem.at[0],
        ),
        pltpu.make_async_copy(table_ref.at[rows(flow)], picks_ref.at[rows(flow)], own_sem.at[1]),
    ]
    for copy in mine:
        copy.start()

    plexes, comps = stoich_ref.shape

    def scalar_products():
        for p in range(plexes):
            for r in range(p + 1):
                for c in range(comps):
                    pairs_ref[(p * plexes + r) * comps + c] = stoich_ref[p, c] * stoich_ref[r, c]

    def entry_weights():
        exact = functools.partial(
            lax.dot_general, precision=lax.Precision.HIGHEST, preferred_element_type=jnp.float32
        )
        wide = exact(table_s_ref[...], across_ref[...], (((0,), (0,)), ((), ())))
        products = exact(first_ref[...], wide, (((1,), (0,)), ((), ())))
        products = products * exact(second_ref[...], wide, (((1,), (0,)), ((), ())))
        place = [lax.rem(lax.broadcasted_iota(jnp.int32, products.shape, k), 8) for k in range(2)]
        products = jnp.where(place[0] == place[1], products, 0.0)
        high = products.astype(jnp.bfloat16).astype(jnp.float32)
        rest = products - high
        middle = rest.astype(jnp.bfloat16).astype(jnp.float32)
        split = jnp.concatenate([high, middle, rest - middle, high, middle], axis=1)
        weights_ref[...] = split.astype(jnp.bfloat16)

    def transport_weights():
        tiles = records // WIN
        left = lax.broadcasted_iota(jnp.int32, (tiles, WIN), 1) < WIN // 2

        def by_tile(ref, view):
            value = ref[...]
            view[...] = jnp.transpose(jnp.concatenate([value, value], axis=0))
            even = view[pl.ds(0, tiles, stride=2), :]
            odd = view[pl.ds(1, tiles, stride=2), :]
            return jnp.where(left, even, odd)

        courant = by_tile(courant_ref, turned_ref)
        scale = 1.0 / (1.0 + courant)
        scale_ref[...] = scale
        weight_ref[...] = courant * scale
        slots_ref[...] = by_tile(slot_ref, index_ref) & (WIN - 1)

    asides = {1: transport_weights, 2: scalar_products, 3: entry_weights}

    def arrival(d, m):
        source = lax.rem(flow + flow_count - d, flow_count)
        owner = lax.rem(rank + members - m, members)
        span = cut(source * capacity + owner * piece, piece)
        return pltpu.make_async_remote_copy(
            src_ref=cells_ref.at[:, span],
            dst_ref=cells_ref.at[:, span],
            send_sem=send_sem.at[m, d],
            recv_sem=recv_sem.at[m, d],
            device_id=others[m - 1] if m else peers[d - 1],
            device_id_type=MESH,
        )

    for d in range(1, flow_count):
        arrival(d, 0).wait_recv()
        source = lax.rem(flow + flow_count - d, flow_count)
        span = cut(source * capacity + rank * piece, piece)
        for m in range(1, members):
            pltpu.make_async_remote_copy(
                src_ref=cells_ref.at[:, span],
                dst_ref=cells_ref.at[:, span],
                send_sem=send_sem.at[m, d],
                recv_sem=recv_sem.at[m, d],
                device_id=others[m - 1],
                device_id_type=MESH,
            ).start()
        if d in asides:
            asides[d]()
    for copy in mine:
        copy.wait()
    for d in range(1, flow_count):
        source = lax.rem(flow + flow_count - d, flow_count)
        pltpu.make_async_remote_copy(
            src_ref=table_ref.at[rows(peers[d - 1][0])],
            dst_ref=picks_ref.at[rows(source)],
            send_sem=pick_send.at[d],
            recv_sem=pick_recv.at[d],
            device_id=peers[d - 1],
            device_id_type=MESH,
        ).wait()
        arrival(d, 0).wait_send()
        for m in range(1, members):
            arrival(d, m).wait()


def forward(stoich, state, pick, slot, courant, sizes):
    flow_count, group_count, parts, members, capacity = sizes
    plexes, comps = stoich.shape
    first, second, across = spread(comps, plexes)
    records = flow_count * capacity
    tiles = records // WIN
    anywhere = pl.BlockSpec(memory_space=pl.ANY)
    vmem = pl.BlockSpec(memory_space=pltpu.VMEM)
    smem = pl.BlockSpec(memory_space=pltpu.SMEM)
    table = jax.ShapeDtypeStruct((tiles, WIN), jnp.float32)
    whole = jax.ShapeDtypeStruct((tiles, WIN), jnp.int32)
    return pl.pallas_call(
        functools.partial(forward_kernel, sizes),
        out_shape=(
            jax.ShapeDtypeStruct((comps, records), jnp.float32),
            whole,
            whole,
            table,
            table,
            jax.ShapeDtypeStruct((plexes * plexes * comps,), jnp.float32),
            jax.ShapeDtypeStruct((first.shape[0], 5 * 8 * plexes), jnp.bfloat16),
        ),
        in_specs=[smem, vmem, vmem, vmem, vmem, anywhere, vmem, vmem, vmem],
        out_specs=(vmem, vmem, vmem, vmem, vmem, smem, vmem),
        scratch_shapes=[
            pltpu.VMEM((tiles, WIN), jnp.int32),
            pltpu.VMEM((2 * tiles, WIN), jnp.float32),
            pltpu.VMEM((2 * tiles, WIN), jnp.int32),
            pltpu.SemaphoreType.DMA((2,)),
            pltpu.SemaphoreType.DMA((members, flow_count)),
            pltpu.SemaphoreType.DMA((members, flow_count)),
            pltpu.SemaphoreType.DMA((flow_count,)),
            pltpu.SemaphoreType.DMA((flow_count,)),
        ],
        compiler_params=pltpu.CompilerParams(
            collective_id=0, has_side_effects=True, vmem_limit_bytes=LIMIT
        ),
    )(stoich, stoich, first, second, across, state, pick, slot, courant)


def react_kernel(
    sizes,
    stoich_ref,
    pairs_ref,
    logk_ref,
    cells_ref,
    pick_ref,
    slot_ref,
    weight_ref,
    scale_ref,
    inflow_ref,
    weights_ref,
    out_ref,
    where_ref,
    matrix_ref,
    moved_ref,
    species_ref,
    sums_ref,
    pair_ref,
    own_sem,
    pair_send,
    pair_recv,
    send_sem,
    recv_sem,
):
    flow_count, group_count, parts, members, capacity = sizes
    comps = cells_ref.shape[0]
    plexes = logk_ref.shape[0]
    width = comps + plexes
    tall = species_ref.shape[0] // (capacity // WIN)
    tiles = pick_ref.shape[0]
    per = capacity // WIN
    half = WIN // 2
    deep = moved_ref.shape[0] // tiles

    flow, group = lax.axis_index("flow"), lax.axis_index("group")
    part, rank = lax.rem(group, parts), lax.div(group, parts)
    share = flow_count * parts // group_count

    def chief_of(which):
        return which * members // parts

    chief = chief_of(part)
    spot = lax.rem(rank + members - chief, members)
    target = part * members + lax.div(flow, share)
    sender = lax.div(group, members)
    sender_group = chief_of(sender) * parts + sender
    sender_flow = lax.rem(group, members) * share
    place = lax.rem(flow, share)

    def column(s):
        return lax.rem(flow + 1 + s, flow_count)

    def to_chief(s, index):
        return pltpu.make_async_remote_copy(
            src_ref=sums_ref.at[column(s)],
            dst_ref=pair_ref.at[index, column(s)],
            send_sem=pair_send.at[s],
            recv_sem=pair_recv.at[index, s],
            device_id=(flow, chief * parts + part),
            device_id_type=MESH,
        )

    def to_owner(s, spot_there):
        return pltpu.make_async_remote_copy(
            src_ref=pair_ref.at[0, column(s)],
            dst_ref=out_ref.at[spot_there],
            send_sem=send_sem.at[s],
            recv_sem=recv_sem.at[spot_there],
            device_id=(column(s), target),
            device_id_type=MESH,
        )

    barrier = pltpu.get_barrier_semaphore()
    for k in range(share):
        source = sender_flow + k

        @pl.when(jnp.logical_or(source != flow, sender_group != group))
        def _():
            pl.semaphore_signal(
                barrier, inc=1, device_id=(source, sender_group), device_id_type=MESH
            )

    @pl.when(spot == 0)
    def _():
        for m in range(1, members):
            pl.semaphore_signal(
                barrier,
                inc=1,
                device_id=(flow, lax.rem(chief + m, members) * parts + part),
                device_id_type=MESH,
            )

    where_ref[...] = jnp.take_along_axis(pick_ref[...] & (WIN - 1), slot_ref[...], axis=1)
    left = lax.broadcasted_iota(jnp.int32, (deep, WIN), 1) < half
    zero = jnp.zeros((deep, WIN), jnp.float32)
    inflow = jnp.concatenate([inflow_ref[...], inflow_ref[...]], axis=1)
    inflow = jnp.concatenate([inflow, zero[comps:]], axis=0)

    def transport(t, carry):
        before_w, before_s, moved = carry
        span = pl.ds(pl.multiple_of(t * WIN, WIN), WIN)
        index = jnp.broadcast_to(where_ref[pl.ds(t, 1), :], (deep, WIN))
        block = jnp.concatenate([cells_ref[:, span], zero[comps:]], axis=0)
        old = jnp.take_along_axis(block, index, axis=1)
        weight = jnp.broadcast_to(weight_ref[pl.ds(t, 1), :], (deep, WIN))
        source = old * jnp.broadcast_to(scale_ref[pl.ds(t, 1), :], (deep, WIN))
        turned_w = pltpu.roll(weight, half, 1)
        turned_s = pltpu.roll(source, half, 1)
        both = weight * jnp.where(left, before_w, turned_w)
        added = weight * jnp.where(left, before_s, turned_s) + source
        moved = both * moved + added
        moved_ref[pl.ds(pl.multiple_of(t * deep, deep), deep), :] = moved
        return turned_w, turned_s, moved

    lax.fori_loop(0, tiles, transport, (zero + 1.0, zero, inflow), unroll=8)

    stoich = [[stoich_ref[p, c] for c in range(comps)] for p in range(plexes)]
    logk = [logk_ref[p] for p in range(plexes)]
    pairs = {}
    for p in range(plexes):
        for r in range(p + 1):
            base = (p * plexes + r) * comps
            pairs[p, r] = [pairs_ref[base + c] for c in range(comps)]
    species_ref[...] = jnp.ones_like(species_ref)
    lanes = lax.broadcasted_iota(jnp.int32, (WIN, WIN), 0)

    def deposit(s):
        for row in range(per):
            value = species_ref[row * tall : (row + 1) * tall, :]
            high = value.astype(jnp.bfloat16).astype(jnp.float32)
            both = jnp.concatenate([high, value - high], axis=0).astype(jnp.bfloat16)
            index = where_ref[pl.ds(column(s) * per + row, 1), :]
            table = jnp.where(lanes == jnp.broadcast_to(index, (WIN, WIN)), 1.0, 0.0)
            sums = lax.dot_general(
                both,
                table.astype(jnp.bfloat16),
                (((1,), (1,)), ((), ())),
                preferred_element_type=jnp.float32,
            )
            total = sums[:tall] + sums[tall:]
            sums_ref[column(s), row * (width + 1) : (row + 1) * (width + 1), :] = total[: width + 1]

    def hand_on(s):
        for index in range(members - 1):

            @pl.when(spot == index + 1)
            def _():
                to_chief(s, index).start()

    def add_up(s):
        for index in range(members - 1):
            to_chief(s, index).wait_recv()
        total = sums_ref[column(s)] + pair_ref[0, column(s)]
        for index in range(1, members - 1):
            total = total + pair_ref[index, column(s)]
        pair_ref[0, column(s)] = total

    def step(s, carry):
        @pl.when(s == 1)
        def _():
            @pl.when(spot != 0)
            def _():
                pl.semaphore_wait(barrier, 1)

            @pl.when(jnp.logical_and(spot == 0, target == group))
            def _():
                pl.semaphore_wait(barrier, flow_count - 1)

            @pl.when(jnp.logical_and(spot == 0, target != group))
            def _():
                pl.semaphore_wait(barrier, flow_count)

        @pl.when(s >= 1)
        def _():
            deposit(s - 1)
            hand_on(s - 1)

        base = column(s) * (per * deep)
        totals = []
        for c in range(comps):
            blocks = [
                moved_ref[pl.ds(base + 8 * k * deep + c, 8, stride=deep), :]
                for k in range(per // 8)
            ]
            totals.append(jnp.concatenate(blocks, axis=1))
        species = newton(totals, stoich, pairs, logk, weights_ref, matrix_ref)
        for q, value in enumerate(species):
            for k in range(per // 8):
                species_ref[pl.ds(8 * k * tall + q, 8, stride=tall), :] = value[
                    :, k * WIN : (k + 1) * WIN
                ]

        @pl.when(jnp.logical_and(s >= 1, spot == 0))
        def _():
            add_up(s - 1)
            to_owner(s - 1, place).start()

        return carry

    lax.fori_loop(0, flow_count, step, 0)
    last = flow_count - 1
    deposit(last)
    hand_on(last)

    @pl.when(spot == 0)
    def _():
        add_up(last)

        @pl.when(target != group)
        def _():
            to_owner(last, place).start()
            to_owner(last, place).wait_send()

        @pl.when(target == group)
        def _():
            copy = pltpu.make_async_copy(pair_ref.at[0, flow], out_ref.at[place], own_sem)
            copy.start()
            copy.wait()

        for s in range(last):
            to_owner(s, place).wait_send()

    @pl.when(spot != 0)
    def _():
        for s in range(flow_count):
            to_chief(s, 0).wait_send()

    for k in range(share):
        source = sender_flow + k

        @pl.when(jnp.logical_or(source != flow, sender_group != group))
        def _():
            to_owner(0, k).wait_recv()


def react(cells, pick, slot, weight, scale, inflow, weights, stoich, pairs, logk, sizes):
    flow_count, group_count, parts, members, capacity = sizes
    comps = cells.shape[0]
    tiles = pick.shape[0]
    per = capacity // WIN
    width = comps + logk.shape[0]
    deep = -(-comps // 8) * 8
    tall = -(-(width + 1) // 8) * 8
    share = flow_count * parts // group_count
    smem = pl.BlockSpec(memory_space=pltpu.SMEM)
    vmem = pl.BlockSpec(memory_space=pltpu.VMEM)
    chunk = (per * (width + 1), WIN)
    return pl.pallas_call(
        functools.partial(react_kernel, sizes),
        out_shape=jax.ShapeDtypeStruct((share,) + chunk, jnp.float32),
        in_specs=[smem] * 3 + [vmem] * 7,
        out_specs=vmem,
        scratch_shapes=[
            pltpu.VMEM((tiles, WIN), jnp.int32),
            pltpu.VMEM((weights.shape[0], per * WIN // 8), jnp.float32),
            pltpu.VMEM((tiles * deep, WIN), jnp.float32),
            pltpu.VMEM((per * tall, WIN), jnp.float32),
            pltpu.VMEM((flow_count,) + chunk, jnp.float32),
            pltpu.VMEM((members - 1, flow_count) + chunk, jnp.float32),
            pltpu.SemaphoreType.DMA,
            pltpu.SemaphoreType.DMA((flow_count,)),
            pltpu.SemaphoreType.DMA((members - 1, flow_count)),
            pltpu.SemaphoreType.DMA((flow_count,)),
            pltpu.SemaphoreType.DMA((share,)),
        ],
        compiler_params=pltpu.CompilerParams(
            collective_id=1, has_side_effects=True, vmem_limit_bytes=LIMIT
        ),
    )(stoich, pairs, logk, cells, pick, slot, weight, scale, inflow, weights)


def mean_kernel(sums_ref, out_ref):
    width = out_ref.shape[0]
    tall = width + 1
    share, height = sums_ref.shape[:2]
    per = height // tall
    for k in range(share):
        for row in range(per):
            value = sums_ref[k, row * tall : row * tall + width, :]
            count = sums_ref[k, row * tall + width : (row + 1) * tall, :]
            tile = k * per + row
            out_ref[:, tile * WIN : (tile + 1) * WIN] = value * (1.0 / jnp.maximum(count, 1.0))


def mean(sums, width):
    share, height = sums.shape[:2]
    vmem = pl.BlockSpec(memory_space=pltpu.VMEM)
    return pl.pallas_call(
        mean_kernel,
        out_shape=jax.ShapeDtypeStruct((width, share * height // (width + 1) * WIN), jnp.float32),
        in_specs=[vmem],
        out_specs=vmem,
        compiler_params=pltpu.CompilerParams(vmem_limit_bytes=LIMIT),
    )(sums)


def body(cell_state, inflow, courant, pick, node_slot, stoich, logk):
    cell_count = cell_state.shape[1]
    flow_count, group_count = lax.axis_size("flow"), lax.axis_size("group")
    capacity = pick.shape[3]
    parts = cell_count // (flow_count * capacity)
    sizes = (flow_count, group_count, parts, group_count // parts, capacity)
    cells, picks, slots, weight, scale, pairs, weights = forward(
        stoich, cell_state, pick.reshape(flow_count, capacity), node_slot.T, courant.T, sizes
    )
    sums = react(cells, picks, slots, weight, scale, inflow, weights, stoich, pairs, logk, sizes)
    return mean(sums, cell_state.shape[0] + logk.shape[0])


def solution(mesh):
    placed = (
        P(None, "flow"),
        P(None, ("flow", "group")),
        P(None, ("flow", "group")),
        P("group", "flow", None, None),
        P(None, ("flow", "group")),
        P(),
        P(),
    )
    return jax.shard_map(
        body, mesh=mesh, in_specs=placed, out_specs=P(None, ("flow", "group")), check_vma=False
    )
```

```python
import functools

import jax
import jax.numpy as jnp
import numpy as np
from jax import lax
from jax.experimental import pallas as pl
from jax.experimental.pallas import tpu as pltpu
from jax.sharding import PartitionSpec as P

ITERS = 4
WIN = 128
LIMIT = 56 * 1024 * 1024
MESH = pl.DeviceIdType.MESH


def blend(factors, values):
    total = factors[0] * values[0]
    for factor, value in zip(factors[1:], values[1:]):
        total = total + factor * value
    return total


def factor_and_solve(matrix, rhs):
    order = len(rhs)
    lower, inverse, middle = {}, [], []
    for p in range(order):
        for r in range(p + 1):
            total = matrix(p, r)
            for o in range(r):
                total = total - lower[p, o] * lower[r, o]
            if p == r:
                inverse.append(lax.rsqrt(total))
            else:
                lower[p, r] = total * inverse[r]
        total = rhs[p]
        for o in range(p):
            total = total - lower[p, o] * middle[o]
        middle.append(total * inverse[p])
    value = [None] * order
    for p in reversed(range(order)):
        total = middle[p]
        for o in range(p + 1, order):
            total = total - lower[o, p] * value[o]
        value[p] = total * inverse[p]
    return value


def entry(p, r):
    return p * (p + 1) // 2 + r


def spread(comps, plexes):
    first = np.zeros((comps * (comps + 1) // 2 * 8, comps), np.float32)
    second = np.zeros_like(first)
    for p in range(comps):
        for r in range(p + 1):
            first[entry(p, r) * 8 : entry(p, r) * 8 + 8, p] = 1.0
            second[entry(p, r) * 8 : entry(p, r) * 8 + 8, r] = 1.0
    across = np.kron(np.eye(plexes, dtype=np.float32), np.ones((1, 8), np.float32))
    return first, second, across


def newton(totals, stoich, pairs, logk, weights_ref, matrix_ref):
    comps, plexes = len(totals), len(logk)
    columns = [[stoich[p][c] for p in range(plexes)] for c in range(comps)]
    logfree = [jnp.log(t) for t in totals]
    over = [1.0 / t for t in totals]
    backs = [jnp.exp(-(logk[p] + blend(stoich[p], logfree))) for p in range(plexes)]

    def small(p, r):
        total = blend(pairs[p, r], over)
        return total + backs[p] if p == r else total

    value = factor_and_solve(small, [jnp.ones_like(totals[0])] * plexes)
    logfree = [x - o * blend(s, value) for x, o, s in zip(logfree, over, columns)]
    for sweep in range(1, ITERS):
        free = [jnp.exp(x) for x in logfree]
        plex = [jnp.exp(logk[p] + blend(stoich[p], logfree)) for p in range(plexes)]
        stack = jnp.concatenate(plex, axis=0)
        high = stack.astype(jnp.bfloat16)
        low = (stack - high.astype(jnp.float32)).astype(jnp.bfloat16)
        parts = jnp.concatenate([high, high, high, low, low], axis=0)
        matrix_ref[...] = jnp.dot(weights_ref[...], parts, preferred_element_type=jnp.float32)
        rhs = [f + blend(s, plex) - t for f, s, t in zip(free, columns, totals)]

        def full(p, r):
            total = matrix_ref[entry(p, r) * 8 : entry(p, r) * 8 + 8, :]
            return total + free[p] if p == r else total

        update = factor_and_solve(full, rhs)
        logfree = [x - u for x, u in zip(logfree, update)]
    plex = [jnp.exp(logk[p] + blend(stoich[p], logfree)) for p in range(plexes)]
    return [jnp.exp(x) for x in logfree] + plex


def partner(index, key, count):
    total, weight = 0, 1
    while weight < count:
        total = total + weight * lax.rem(lax.div(index, weight) + key // weight % 2, 2)
        weight *= 2
    return total


def forward_kernel(
    sizes,
    stoich_ref,
    table_s_ref,
    first_ref,
    second_ref,
    across_ref,
    state_ref,
    pick_ref,
    slot_ref,
    courant_ref,
    cells_ref,
    picks_ref,
    slots_ref,
    weight_ref,
    scale_ref,
    pairs_ref,
    weights_ref,
    table_ref,
    turned_ref,
    index_ref,
    own_sem,
    send_sem,
    recv_sem,
    pick_send,
    pick_recv,
):
    flow_count, group_count, parts, members, capacity = sizes
    flow, group = lax.axis_index("flow"), lax.axis_index("group")
    part, rank = lax.rem(group, parts), lax.div(group, parts)
    records = flow_count * capacity
    piece = capacity // members
    others = [
        (flow, lax.rem(rank + m, members) * parts + part) for m in range(1, members)
    ]
    peers = [(partner(flow, d, flow_count), group) for d in range(1, flow_count)]
    barrier = pltpu.get_barrier_semaphore()
    for peer in others + peers:
        pl.semaphore_signal(barrier, inc=1, device_id=peer, device_id_type=MESH)
    per = capacity // WIN
    for k in range(per):
        table_ref[pl.ds(k, flow_count, stride=per), :] = pick_ref[:, k * WIN : (k + 1) * WIN]
    pl.semaphore_wait(barrier, len(others) + len(peers))

    def cut(start, size):
        return pl.ds(pl.multiple_of(start, WIN), size)

    def rows(index):
        return pl.ds(pl.multiple_of(index * per, per), per)

    first = part * records
    for d in range(1, flow_count):
        peer = peers[d - 1]
        pltpu.make_async_remote_copy(
            src_ref=state_ref.at[:, cut(first + peer[0] * capacity + rank * piece, piece)],
            dst_ref=cells_ref.at[:, cut(flow * capacity + rank * piece, piece)],
            send_sem=send_sem.at[0, d],
            recv_sem=recv_sem.at[0, d],
            device_id=peer,
            device_id_type=MESH,
        ).start()
    for d in range(1, flow_count):
        peer = peers[d - 1]
        pltpu.make_async_remote_copy(
            src_ref=table_ref.at[rows(peer[0])],
            dst_ref=picks_ref.at[rows(flow)],
            send_sem=pick_send.at[d],
            recv_sem=pick_recv.at[d],
            device_id=peer,
            device_id_type=MESH,
        ).start()
    mine = [
        pltpu.make_async_copy(
            state_ref.at[:, cut(first + flow * capacity, capacity)],
            cells_ref.at[:, cut(flow * capacity, capacity)],
            own_sem.at[0],
        ),
        pltpu.make_async_copy(table_ref.at[rows(flow)], picks_ref.at[rows(flow)], own_sem.at[1]),
    ]
    for copy in mine:
        copy.start()

    plexes, comps = stoich_ref.shape

    def scalar_products():
        for p in range(plexes):
            for r in range(p + 1):
                for c in range(comps):
                    pairs_ref[(p * plexes + r) * comps + c] = stoich_ref[p, c] * stoich_ref[r, c]

    def entry_weights():
        exact = functools.partial(
            lax.dot_general, precision=lax.Precision.HIGHEST, preferred_element_type=jnp.float32
        )
        wide = exact(table_s_ref[...], across_ref[...], (((0,), (0,)), ((), ())))
        products = exact(first_ref[...], wide, (((1,), (0,)), ((), ())))
        products = products * exact(second_ref[...], wide, (((1,), (0,)), ((), ())))
        place = [lax.rem(lax.broadcasted_iota(jnp.int32, products.shape, k), 8) for k in range(2)]
        products = jnp.where(place[0] == place[1], products, 0.0)
        high = products.astype(jnp.bfloat16).astype(jnp.float32)
        rest = products - high
        middle = rest.astype(jnp.bfloat16).astype(jnp.float32)
        split = jnp.concatenate([high, middle, rest - middle, high, middle], axis=1)
        weights_ref[...] = split.astype(jnp.bfloat16)

    def transport_weights():
        tiles = records // WIN
        left = lax.broadcasted_iota(jnp.int32, (tiles, WIN), 1) < WIN // 2

        def by_tile(ref, view):
            value = ref[...]
            view[...] = jnp.transpose(jnp.concatenate([value, value], axis=0))
            even = view[pl.ds(0, tiles, stride=2), :]
            odd = view[pl.ds(1, tiles, stride=2), :]
            return jnp.where(left, even, odd)

        courant = by_tile(courant_ref, turned_ref)
        scale = 1.0 / (1.0 + courant)
        scale_ref[...] = scale
        weight_ref[...] = courant * scale
        slots_ref[...] = by_tile(slot_ref, index_ref) & (WIN - 1)

    asides = {1: transport_weights, 2: scalar_products, 3: entry_weights}

    def arrival(d, m):
        source = peers[d - 1][0]
        owner = lax.rem(rank + members - m, members)
        span = cut(source * capacity + owner * piece, piece)
        return pltpu.make_async_remote_copy(
            src_ref=cells_ref.at[:, span],
            dst_ref=cells_ref.at[:, span],
            send_sem=send_sem.at[m, d],
            recv_sem=recv_sem.at[m, d],
            device_id=others[m - 1] if m else peers[d - 1],
            device_id_type=MESH,
        )

    for d in range(1, flow_count):
        arrival(d, 0).wait_recv()
        source = peers[d - 1][0]
        span = cut(source * capacity + rank * piece, piece)
        for m in range(1, members):
            pltpu.make_async_remote_copy(
                src_ref=cells_ref.at[:, span],
                dst_ref=cells_ref.at[:, span],
                send_sem=send_sem.at[m, d],
                recv_sem=recv_sem.at[m, d],
                device_id=others[m - 1],
                device_id_type=MESH,
            ).start()
        if d in asides:
            asides[d]()
    for copy in mine:
        copy.wait()
    for d in range(1, flow_count):
        source = peers[d - 1][0]
        pltpu.make_async_remote_copy(
            src_ref=table_ref.at[rows(peers[d - 1][0])],
            dst_ref=picks_ref.at[rows(source)],
            send_sem=pick_send.at[d],
            recv_sem=pick_recv.at[d],
            device_id=peers[d - 1],
            device_id_type=MESH,
        ).wait()
        arrival(d, 0).wait_send()
        for m in range(1, members):
            arrival(d, m).wait()


def forward(stoich, state, pick, slot, courant, sizes):
    flow_count, group_count, parts, members, capacity = sizes
    plexes, comps = stoich.shape
    first, second, across = spread(comps, plexes)
    records = flow_count * capacity
    tiles = records // WIN
    anywhere = pl.BlockSpec(memory_space=pl.ANY)
    vmem = pl.BlockSpec(memory_space=pltpu.VMEM)
    smem = pl.BlockSpec(memory_space=pltpu.SMEM)
    table = jax.ShapeDtypeStruct((tiles, WIN), jnp.float32)
    whole = jax.ShapeDtypeStruct((tiles, WIN), jnp.int32)
    return pl.pallas_call(
        functools.partial(forward_kernel, sizes),
        out_shape=(
            jax.ShapeDtypeStruct((comps, records), jnp.float32),
            whole,
            whole,
            table,
            table,
            jax.ShapeDtypeStruct((plexes * plexes * comps,), jnp.float32),
            jax.ShapeDtypeStruct((first.shape[0], 5 * 8 * plexes), jnp.bfloat16),
        ),
        in_specs=[smem, vmem, vmem, vmem, vmem, anywhere, vmem, vmem, vmem],
        out_specs=(vmem, vmem, vmem, vmem, vmem, smem, vmem),
        scratch_shapes=[
            pltpu.VMEM((tiles, WIN), jnp.int32),
            pltpu.VMEM((2 * tiles, WIN), jnp.float32),
            pltpu.VMEM((2 * tiles, WIN), jnp.int32),
            pltpu.SemaphoreType.DMA((2,)),
            pltpu.SemaphoreType.DMA((members, flow_count)),
            pltpu.SemaphoreType.DMA((members, flow_count)),
            pltpu.SemaphoreType.DMA((flow_count,)),
            pltpu.SemaphoreType.DMA((flow_count,)),
        ],
        compiler_params=pltpu.CompilerParams(
            collective_id=0, has_side_effects=True, vmem_limit_bytes=LIMIT
        ),
    )(stoich, stoich, first, second, across, state, pick, slot, courant)


def react_kernel(
    sizes,
    stoich_ref,
    pairs_ref,
    logk_ref,
    cells_ref,
    pick_ref,
    slot_ref,
    weight_ref,
    scale_ref,
    inflow_ref,
    weights_ref,
    out_ref,
    where_ref,
    matrix_ref,
    moved_ref,
    species_ref,
    sums_ref,
    pair_ref,
    own_sem,
    pair_send,
    pair_recv,
    send_sem,
    recv_sem,
):
    flow_count, group_count, parts, members, capacity = sizes
    comps = cells_ref.shape[0]
    plexes = logk_ref.shape[0]
    width = comps + plexes
    tall = species_ref.shape[0] // (capacity // WIN)
    tiles = pick_ref.shape[0]
    per = capacity // WIN
    half = WIN // 2
    deep = moved_ref.shape[0] // tiles

    flow, group = lax.axis_index("flow"), lax.axis_index("group")
    part, rank = lax.rem(group, parts), lax.div(group, parts)
    share = flow_count * parts // group_count

    def chief_of(which):
        return which * members // parts

    chief = chief_of(part)
    spot = lax.rem(rank + members - chief, members)
    target = part * members + lax.div(flow, share)
    sender = lax.div(group, members)
    sender_group = chief_of(sender) * parts + sender
    sender_flow = lax.rem(group, members) * share
    place = lax.rem(flow, share)

    def column(s):
        return partner(flow, flow_count - 1 - s, flow_count)

    def to_chief(s, index):
        return pltpu.make_async_remote_copy(
            src_ref=sums_ref.at[column(s)],
            dst_ref=pair_ref.at[index, column(s)],
            send_sem=pair_send.at[s],
            recv_sem=pair_recv.at[index, s],
            device_id=(flow, chief * parts + part),
            device_id_type=MESH,
        )

    def to_owner(s, spot_there):
        return pltpu.make_async_remote_copy(
            src_ref=pair_ref.at[0, column(s)],
            dst_ref=out_ref.at[spot_there],
            send_sem=send_sem.at[s],
            recv_sem=recv_sem.at[spot_there],
            device_id=(column(s), target),
            device_id_type=MESH,
        )

    barrier = pltpu.get_barrier_semaphore()
    for k in range(share):
        source = sender_flow + k

        @pl.when(jnp.logical_or(source != flow, sender_group != group))
        def _():
            pl.semaphore_signal(
                barrier, inc=1, device_id=(source, sender_group), device_id_type=MESH
            )

    @pl.when(spot == 0)
    def _():
        for m in range(1, members):
            pl.semaphore_signal(
                barrier,
                inc=1,
                device_id=(flow, lax.rem(chief + m, members) * parts + part),
                device_id_type=MESH,
            )

    where_ref[...] = jnp.take_along_axis(pick_ref[...] & (WIN - 1), slot_ref[...], axis=1)
    left = lax.broadcasted_iota(jnp.int32, (deep, WIN), 1) < half
    zero = jnp.zeros((deep, WIN), jnp.float32)
    inflow = jnp.concatenate([inflow_ref[...], inflow_ref[...]], axis=1)
    inflow = jnp.concatenate([inflow, zero[comps:]], axis=0)

    def transport(t, carry):
        before_w, before_s, moved = carry
        span = pl.ds(pl.multiple_of(t * WIN, WIN), WIN)
        index = jnp.broadcast_to(where_ref[pl.ds(t, 1), :], (deep, WIN))
        block = jnp.concatenate([cells_ref[:, span], zero[comps:]], axis=0)
        old = jnp.take_along_axis(block, index, axis=1)
        weight = jnp.broadcast_to(weight_ref[pl.ds(t, 1), :], (deep, WIN))
        source = old * jnp.broadcast_to(scale_ref[pl.ds(t, 1), :], (deep, WIN))
        turned_w = pltpu.roll(weight, half, 1)
        turned_s = pltpu.roll(source, half, 1)
        both = weight * jnp.where(left, before_w, turned_w)
        added = weight * jnp.where(left, before_s, turned_s) + source
        moved = both * moved + added
        moved_ref[pl.ds(pl.multiple_of(t * deep, deep), deep), :] = moved
        return turned_w, turned_s, moved

    lax.fori_loop(0, tiles, transport, (zero + 1.0, zero, inflow), unroll=8)

    stoich = [[stoich_ref[p, c] for c in range(comps)] for p in range(plexes)]
    logk = [logk_ref[p] for p in range(plexes)]
    pairs = {}
    for p in range(plexes):
        for r in range(p + 1):
            base = (p * plexes + r) * comps
            pairs[p, r] = [pairs_ref[base + c] for c in range(comps)]
    species_ref[...] = jnp.ones_like(species_ref)
    lanes = lax.broadcasted_iota(jnp.int32, (WIN, WIN), 0)

    def deposit(s):
        for row in range(per):
            value = species_ref[row * tall : (row + 1) * tall, :]
            high = value.astype(jnp.bfloat16).astype(jnp.float32)
            both = jnp.concatenate([high, value - high], axis=0).astype(jnp.bfloat16)
            index = where_ref[pl.ds(column(s) * per + row, 1), :]
            table = jnp.where(lanes == jnp.broadcast_to(index, (WIN, WIN)), 1.0, 0.0)
            sums = lax.dot_general(
                both,
                table.astype(jnp.bfloat16),
                (((1,), (1,)), ((), ())),
                preferred_element_type=jnp.float32,
            )
            total = sums[:tall] + sums[tall:]
            sums_ref[column(s), row * (width + 1) : (row + 1) * (width + 1), :] = total[: width + 1]

    def hand_on(s):
        for index in range(members - 1):

            @pl.when(spot == index + 1)
            def _():
                to_chief(s, index).start()

    def add_up(s):
        for index in range(members - 1):
            to_chief(s, index).wait_recv()
        total = sums_ref[column(s)] + pair_ref[0, column(s)]
        for index in range(1, members - 1):
            total = total + pair_ref[index, column(s)]
        pair_ref[0, column(s)] = total

    def step(s, carry):
        @pl.when(s == 1)
        def _():
            @pl.when(spot != 0)
            def _():
                pl.semaphore_wait(barrier, 1)

            @pl.when(jnp.logical_and(spot == 0, target == group))
            def _():
                pl.semaphore_wait(barrier, flow_count - 1)

            @pl.when(jnp.logical_and(spot == 0, target != group))
            def _():
                pl.semaphore_wait(barrier, flow_count)

        @pl.when(s >= 1)
        def _():
            deposit(s - 1)
            hand_on(s - 1)

        base = column(s) * (per * deep)
        totals = []
        for c in range(comps):
            blocks = [
                moved_ref[pl.ds(base + 8 * k * deep + c, 8, stride=deep), :]
                for k in range(per // 8)
            ]
            totals.append(jnp.concatenate(blocks, axis=1))
        species = newton(totals, stoich, pairs, logk, weights_ref, matrix_ref)
        for q, value in enumerate(species):
            for k in range(per // 8):
                species_ref[pl.ds(8 * k * tall + q, 8, stride=tall), :] = value[
                    :, k * WIN : (k + 1) * WIN
                ]

        @pl.when(jnp.logical_and(s >= 1, spot == 0))
        def _():
            add_up(s - 1)
            to_owner(s - 1, place).start()

        return carry

    lax.fori_loop(0, flow_count, step, 0)
    last = flow_count - 1
    deposit(last)
    hand_on(last)

    @pl.when(spot == 0)
    def _():
        add_up(last)

        @pl.when(target != group)
        def _():
            to_owner(last, place).start()
            to_owner(last, place).wait_send()

        @pl.when(target == group)
        def _():
            copy = pltpu.make_async_copy(pair_ref.at[0, flow], out_ref.at[place], own_sem)
            copy.start()
            copy.wait()

        for s in range(last):
            to_owner(s, place).wait_send()

    @pl.when(spot != 0)
    def _():
        for s in range(flow_count):
            to_chief(s, 0).wait_send()

    for k in range(share):
        source = sender_flow + k

        @pl.when(jnp.logical_or(source != flow, sender_group != group))
        def _():
            to_owner(0, k).wait_recv()


def react(cells, pick, slot, weight, scale, inflow, weights, stoich, pairs, logk, sizes):
    flow_count, group_count, parts, members, capacity = sizes
    comps = cells.shape[0]
    tiles = pick.shape[0]
    per = capacity // WIN
    width = comps + logk.shape[0]
    deep = -(-comps // 8) * 8
    tall = -(-(width + 1) // 8) * 8
    share = flow_count * parts // group_count
    smem = pl.BlockSpec(memory_space=pltpu.SMEM)
    vmem = pl.BlockSpec(memory_space=pltpu.VMEM)
    chunk = (per * (width + 1), WIN)
    return pl.pallas_call(
        functools.partial(react_kernel, sizes),
        out_shape=jax.ShapeDtypeStruct((share,) + chunk, jnp.float32),
        in_specs=[smem] * 3 + [vmem] * 7,
        out_specs=vmem,
        scratch_shapes=[
            pltpu.VMEM((tiles, WIN), jnp.int32),
            pltpu.VMEM((weights.shape[0], per * WIN // 8), jnp.float32),
            pltpu.VMEM((tiles * deep, WIN), jnp.float32),
            pltpu.VMEM((per * tall, WIN), jnp.float32),
            pltpu.VMEM((flow_count,) + chunk, jnp.float32),
            pltpu.VMEM((members - 1, flow_count) + chunk, jnp.float32),
            pltpu.SemaphoreType.DMA,
            pltpu.SemaphoreType.DMA((flow_count,)),
            pltpu.SemaphoreType.DMA((members - 1, flow_count)),
            pltpu.SemaphoreType.DMA((flow_count,)),
            pltpu.SemaphoreType.DMA((share,)),
        ],
        compiler_params=pltpu.CompilerParams(
            collective_id=1, has_side_effects=True, vmem_limit_bytes=LIMIT
        ),
    )(stoich, pairs, logk, cells, pick, slot, weight, scale, inflow, weights)


def mean_kernel(sums_ref, out_ref):
    width = out_ref.shape[0]
    tall = width + 1
    share, height = sums_ref.shape[:2]
    per = height // tall
    for k in range(share):
        for row in range(per):
            value = sums_ref[k, row * tall : row * tall + width, :]
            count = sums_ref[k, row * tall + width : (row + 1) * tall, :]
            tile = k * per + row
            out_ref[:, tile * WIN : (tile + 1) * WIN] = value * (1.0 / jnp.maximum(count, 1.0))


def mean(sums, width):
    share, height = sums.shape[:2]
    vmem = pl.BlockSpec(memory_space=pltpu.VMEM)
    return pl.pallas_call(
        mean_kernel,
        out_shape=jax.ShapeDtypeStruct((width, share * height // (width + 1) * WIN), jnp.float32),
        in_specs=[vmem],
        out_specs=vmem,
        compiler_params=pltpu.CompilerParams(vmem_limit_bytes=LIMIT),
    )(sums)


def body(cell_state, inflow, courant, pick, node_slot, stoich, logk):
    cell_count = cell_state.shape[1]
    flow_count, group_count = lax.axis_size("flow"), lax.axis_size("group")
    capacity = pick.shape[3]
    parts = cell_count // (flow_count * capacity)
    sizes = (flow_count, group_count, parts, group_count // parts, capacity)
    cells, picks, slots, weight, scale, pairs, weights = forward(
        stoich, cell_state, pick.reshape(flow_count, capacity), node_slot.T, courant.T, sizes
    )
    sums = react(cells, picks, slots, weight, scale, inflow, weights, stoich, pairs, logk, sizes)
    return mean(sums, cell_state.shape[0] + logk.shape[0])


def solution(mesh):
    placed = (
        P(None, "flow"),
        P(None, ("flow", "group")),
        P(None, ("flow", "group")),
        P("group", "flow", None, None),
        P(None, ("flow", "group")),
        P(),
        P(),
    )
    return jax.shard_map(
        body, mesh=mesh, in_specs=placed, out_specs=P(None, ("flow", "group")), check_vma=False
    )
```
